256 devices in a mesh: dp: 32 (over y, x, core), expert: 8 (over z).
Axes of the slice: x: 4, y: 4, z: 8, core: 2. Of those that a mesh axis runs over, the one named last changes fastest.
Arguments:
- hidden_in: bfloat16 [32768, 2048], P(('dp', 'expert')), may hold values from -6 to 6
- resid_in: bfloat16 [32768, 2048], P(('dp', 'expert')), may hold values from -12 to 12
- route_ids: int32 [32768, 2], P(('dp', 'expert')), may hold values from 0 to 7, all different within a row; in each aligned block of 128 rows (0 to 127, 128 to 255, ...) at most 48 rows name the same one
- route_weight: float32 [32768, 2], P(('dp', 'expert')), may hold values from 0.05 to 0.6
- returns: float32 [32768], P(('dp', 'expert')), may hold values from -40 to 50
- run_moments: float32 [2], replicated, may hold values from 0.5 to 2
- gate_w: bfloat16 [8, 2048, 768], P('expert'), may hold values from -0.125 to 0.125
- up_w: bfloat16 [8, 2048, 768], P('expert'), may hold values from -0.125 to 0.125
- down_w: bfloat16 [8, 768, 2048], P('expert'), may hold values from -0.21875 to 0.21875
- value_w: bfloat16 [2048, 256], replicated
Outputs:
- grad_hidden: bfloat16 [32768, 2048], P(('dp', 'expert'))
- grad_route: float32 [32768, 2], P(('dp', 'expert'))
- grad_gate: float32 [8, 2048, 768], P('expert', 'dp')
- grad_up: float32 [8, 2048, 768], P('expert', 'dp')
- grad_down: float32 [8, 768, 2048], P('expert', None, 'dp')
- grad_value: float32 [2048, 256], P(('dp', 'expert'))
The draws below stay inside these ranges and needn't reach their ends.
Inputs may be any that keep to these rules, and one draw needn't show every extreme that they name: `route_ids`: each token names 2 different experts. Among the routes of one device no expert is named more than 48 times, and in every draw some device names some expert exactly 48 times.
All inputs are finite; a program needn't handle non-finite values.
Results may differ from the reference program's by a relative error of at most 0.024.
Values may be sent and summed in bfloat16 or wider, within the bound.
No kernel may reach another device: no remote copies, remote signals or barrier semaphores. Data moves between devices by JAX's collectives and lax.ppermute only.
A program may use at most 128 MiB of HBM per device.

```python
import math
import jax
import jax.numpy as jnp
import numpy as np
from jax import lax

D = 2048
FF = 768
BINS = 256
ROUTES = 2
TOK_DEV = 128
EXPERTS = 8
CAP = 48
TOKENS = 32768
N_DP = 32


def head_table(key):
    normal_part = jax.random.truncated_normal(key, -4.0, 4.0, (D, BINS), jnp.float32)
    return normal_part * (3.0 / math.sqrt(D))


def draw_value_w(key, part):
    columns = head_table(key)
    return columns.astype(jnp.bfloat16)


def block_boost(key, factor):
    device_count = TOKENS // TOK_DEV
    block_width = D // device_count
    table = jax.random.randint(key, (device_count, device_count), 0, 8) == 0
    row_device = (jnp.arange(TOKENS) // TOK_DEV)[:, None]
    col_block = (jnp.arange(D) // block_width)[None, :]
    marked = table[row_device, col_block]
    return jnp.where(marked, factor, 1.0).astype(jnp.float32)


def draw_resid_in(key, part):
    key = jax.random.fold_in(key, 2)
    key_base = jax.random.fold_in(key, 0)
    key_boost = jax.random.fold_in(key, 4)
    boost = block_boost(key_boost, 3.0)
    values = jnp.clip(jax.random.truncated_normal(key_base, -6.0, 6.0, (TOKENS, D), jnp.float32) * boost, -12.0, 12.0)
    return values.astype(jnp.bfloat16)


def draw_returns(key, part):
    key = jax.random.fold_in(key, 3)
    key_noise = jax.random.fold_in(key, 0)
    position_frac = jnp.arange(TOKENS).astype(jnp.float32) / TOKENS
    row_scale = jnp.exp(math.log(10.0) * position_frac)
    jitter = jax.random.truncated_normal(key_noise, -4.0, 4.0, (TOKENS,), jnp.float32)
    values = 2.0 + 4.0 * position_frac + row_scale * jitter
    return values


def block_levels(own_key, extent, cuts, low, high):
    factor_of, own = 1.0, jax.random.fold_in(own_key, 6)
    for dim, blocks in cuts:
        draws = jnp.exp(jax.random.uniform(jax.random.fold_in(own, dim), (blocks,), jnp.float32, low / len(cuts), high / len(cuts)))
        factor_of = factor_of * jnp.repeat(draws, extent[dim] // blocks).reshape([-1 if axis == dim else 1 for axis in range(len(extent))])
    return factor_of


def routed_block(key, own, number, rows, count, top, reach, slope):
    order = jax.random.permutation(key, count)
    crowded, usual = load_shares(count, rows * top, reach, slope, True), load_shares(count, rows * top, reach, slope, False)
    places = jnp.arange(count)

    def named(lengths, turn):
        used = int((lengths > 0).sum())
        fixed = max(1, used // 4)
        passed = fixed + (places - fixed + turn * (used - fixed)) % max(1, count - fixed)
        return jnp.zeros((count,), jnp.int32).at[order[jnp.where(places < fixed, places, passed)]].set(jnp.asarray(lengths, jnp.int32))

    lengths = jnp.where(number % 4 == 0, named(crowded, number // 4), named(usual, number - number // 4 - 1))
    mixed = jax.random.permutation(jax.random.fold_in(own, 3), count)
    source_of, receiver = mixed[0:count // 2 * 2:2], mixed[1:count // 2 * 2:2]
    margin = jnp.minimum(lengths[source_of] - 1, reach - lengths[receiver]) // 2
    margin = jnp.where((source_of == order[0]) | (receiver == order[0]) | (lengths[receiver] == 0), 0, jnp.maximum(margin, 0))
    passed = jax.random.randint(jax.random.fold_in(own, 4), (count // 2,), 0, 1 << 20) % (margin + 1)
    lengths = lengths.at[source_of].add(-passed).at[receiver].add(passed)
    items = jnp.searchsorted(jnp.cumsum(lengths), jnp.arange(rows * top), side="right").astype(jnp.int32)
    grid = items.reshape(top, rows).T
    grid = grid[jax.random.permutation(jax.random.fold_in(own, 1), rows)]
    turn = jax.random.randint(jax.random.fold_in(own, 2), (rows, 1), 0, top)
    return jnp.take_along_axis(grid, (jnp.arange(top)[None, :] + turn) % top, axis=1)


def load_shares(number_of, total, most, slope, full):
    portions = [(1 << 20) // math.isqrt(rank ** slope) + 1 for rank in range(1, number_of + 1)]
    largest = most if full else min(most, max(-(-total // number_of), total * portions[0] // sum(portions)))
    least = 1 if total - largest >= number_of - 1 else 0
    holding, spare = [largest] + [least] * (number_of - 1), total - largest - least * (number_of - 1)
    while spare > 0:
        candidates = [i for i in range(1, number_of) if holding[i] < largest] or [i for i in range(1, number_of) if holding[i] < most]
        mass, remaining = sum([portions[i] for i in candidates]), spare
        for i in candidates:
            more = min(most - holding[i], max(1, remaining * portions[i] // mass), spare)
            holding[i] = holding[i] + more
            spare = spare - more
    return np.array(holding)


def noise(key, shape, deviation, limit, cuts=(), held_as=jnp.bfloat16):
    entries = jax.random.normal(key, shape, jnp.float32) * deviation
    if len(cuts) > 0:
        entries = block_levels(key, shape, cuts, -0.22, 0.18) * entries
    return jnp.clip(entries, min=-limit, max=limit).astype(held_as)


def setup_inputs(seed: int = 0) -> dict:
    keys = jax.random.split(jax.random.key(seed), 11)
    hidden_in = noise(keys[0], (TOKENS, D), 1.0, 6.0, ((0, 256),))
    resid_in = draw_resid_in(jax.random.fold_in(keys[10], 71), 0)
    route_ids_keys = jax.random.split(jax.random.fold_in(keys[2], 1), TOKENS // TOK_DEV)
    route_ids_turns = jax.random.permutation(jax.random.fold_in(keys[2], 3), TOKENS // TOK_DEV)
    route_ids = jax.vmap(lambda own, number: routed_block(jax.random.fold_in(keys[2], 2), own, number, TOK_DEV, EXPERTS, ROUTES, CAP, 2))(route_ids_keys, route_ids_turns).reshape((TOKENS, ROUTES))
    route_weight = jnp.clip(jnp.exp(math.log(0.6) - 2.4849067 * jax.random.uniform(keys[3], (TOKENS, ROUTES), jnp.float32) ** block_levels(keys[3], (TOKENS, ROUTES), ((0, 256),), -0.2, 0.2)), 0.05, 0.6)
    returns = draw_returns(jax.random.fold_in(keys[10], 71), 0)
    run_moments = jnp.clip(jax.random.uniform(keys[5], (2,), jnp.float32, 0.5, 2.0), 0.5, 2.0)
    gate_w = noise(keys[6], (EXPERTS, D, FF), D ** -0.5, 0.125, ((0, 8),))
    up_w = noise(keys[7], (EXPERTS, D, FF), D ** -0.5, 0.125, ((0, 8),))
    down_w = noise(keys[8], (EXPERTS, FF, D), FF ** -0.5, 0.21875, ((0, 8),))
    value_w = draw_value_w(jax.random.fold_in(keys[10], 71), 0)
    return {"hidden_in": hidden_in, "resid_in": resid_in, "route_ids": route_ids, "route_weight": route_weight, "returns": returns, "run_moments": run_moments, "gate_w": gate_w, "up_w": up_w, "down_w": down_w, "value_w": value_w}


support_edge = 4.0
smoothing = 0.75

def hl_targets(returns, mean_value, var_value):
    scaled = jnp.clip((returns - mean_value) / jnp.sqrt(var_value + 1e-06), -support_edge, support_edge)
    bin_edges = -support_edge + 2.0 * support_edge / BINS * jnp.arange(BINS + 1).astype(jnp.float32)
    bin_sigma = smoothing * 2.0 * support_edge / BINS
    cumulative = jax.scipy.special.erf((bin_edges[None, :] - scaled[:, None]) / (math.sqrt(2.0) * bin_sigma))
    bin_mass = cumulative[:, 1:] - cumulative[:, :-1]
    return bin_mass / (cumulative[:, -1:] - cumulative[:, :1])

def group_slots(id_group):
    blocks = id_group.reshape(EXPERTS, TOK_DEV * ROUTES)
    onehot = (blocks[:, :, None] == jnp.arange(EXPERTS).astype(jnp.int32)[None, None, :]).astype(jnp.int32)
    position = lax.optimization_barrier(jnp.sum((jnp.cumsum(onehot, axis=1) - onehot) * onehot, axis=2))
    source = jnp.arange(EXPERTS).astype(jnp.int32)[:, None]
    slot_index = (blocks * (EXPERTS * CAP) + source * CAP + position).reshape(-1).astype(jnp.int32)
    slot_total = EXPERTS * EXPERTS * CAP
    route_order = jnp.arange(slot_index.shape[0]).astype(jnp.int32)
    slot_route = jnp.zeros((slot_total,), jnp.int32).at[slot_index].set(route_order)
    slot_live = jnp.zeros((slot_total,), jnp.int32).at[slot_index].set(1) > 0
    return (slot_index, slot_route, slot_live)

def slot_rows(source_rows, index, slot_live):
    picked = jnp.where(slot_live[:, None], source_rows[index], jnp.zeros((), source_rows.dtype))
    return picked.reshape(EXPERTS, EXPERTS * CAP, D)

def expert_front(in_rows, gate_w, up_w):
    gate_pre = jnp.einsum('esd,edf->esf', in_rows.astype(jnp.float32), gate_w.astype(jnp.float32))
    up_pre = jnp.einsum('esd,edf->esf', in_rows.astype(jnp.float32), up_w.astype(jnp.float32))
    gate_sig = jax.nn.sigmoid(gate_pre)
    activation = (gate_pre * gate_sig * up_pre).astype(jnp.bfloat16)
    return (gate_pre, up_pre, gate_sig, activation)

def rounded_add(total, term):
    return total + lax.optimization_barrier(term.astype(jnp.bfloat16)).astype(jnp.float32)

def reference(hidden_in, resid_in, route_ids, route_weight, returns, run_moments, gate_w, up_w, down_w, value_w):
    batch_mean = jnp.mean(returns)
    batch_var = jnp.mean((returns - batch_mean) ** 2)
    mean_value = 0.5 * (run_moments[0] + batch_mean)
    var_value = 0.5 * (run_moments[1] + batch_var) + 0.25 * (batch_mean - run_moments[0]) ** 2
    targets = hl_targets(returns, mean_value, var_value)
    group_rows = EXPERTS * TOK_DEV
    slot_total = EXPERTS * EXPERTS * CAP
    hidden_groups = hidden_in.reshape(N_DP, group_rows, D)
    id_groups = route_ids.reshape(N_DP, group_rows, ROUTES)

    def forward_group(operands):
        hidden_group, id_group = operands
        slot_index, slot_route, slot_live = group_slots(id_group)
        in_rows = slot_rows(hidden_group, slot_route // ROUTES, slot_live)
        gate_pre, up_pre, gate_sig, activation = expert_front(in_rows, gate_w, up_w)
        expert_out = jnp.einsum('esf,efd->esd', activation.astype(jnp.float32), down_w.astype(jnp.float32)).astype(jnp.bfloat16)
        return expert_out.reshape(slot_total, D)[slot_index].reshape(group_rows, ROUTES, D)
    route_out = lax.map(forward_group, (hidden_groups, id_groups)).reshape(TOKENS, ROUTES, D)
    route_f = route_out.astype(jnp.float32)
    stream = resid_in.astype(jnp.float32) + jnp.einsum('tk,tkd->td', route_weight, route_f)
    features = stream.astype(jnp.bfloat16)
    logits = jnp.dot(features, value_w, preferred_element_type=jnp.float32)
    softmax_p = jax.nn.softmax(logits, axis=-1)
    logit_grad = (softmax_p - targets).astype(jnp.bfloat16)
    feature_grad = jnp.dot(logit_grad, value_w.T, preferred_element_type=jnp.float32)
    grad_route = jnp.einsum('tkd,td->tk', route_f, feature_grad)
    route_grad = (route_weight[:, :, None] * feature_grad[:, None, :]).astype(jnp.bfloat16)
    grad_groups = route_grad.reshape(N_DP, group_rows * ROUTES, D)
    grad_value = jnp.dot(features.T, logit_grad, preferred_element_type=jnp.float32)

    def backward_group(carry, operands):
        hidden_group, id_group, grad_group = operands
        slot_index, slot_route, slot_live = group_slots(id_group)
        in_rows = slot_rows(hidden_group, slot_route // ROUTES, slot_live)
        grad_rows = slot_rows(grad_group, slot_route, slot_live)
        gate_pre, up_pre, gate_sig, activation = expert_front(in_rows, gate_w, up_w)
        act_grad = jnp.einsum('esd,efd->esf', grad_rows.astype(jnp.float32), down_w.astype(jnp.float32))
        gate_grad = (act_grad * up_pre * gate_sig * (1.0 + gate_pre * (1.0 - gate_sig))).astype(jnp.bfloat16)
        up_grad = (act_grad * gate_pre * gate_sig).astype(jnp.bfloat16)
        input_grad = (jnp.einsum('esf,edf->esd', gate_grad.astype(jnp.float32), gate_w.astype(jnp.float32)) + jnp.einsum('esf,edf->esd', up_grad.astype(jnp.float32), up_w.astype(jnp.float32))).astype(jnp.bfloat16)
        route_back = input_grad.reshape(slot_total, D)[slot_index].reshape(group_rows, ROUTES, D)
        hidden_grad = lax.optimization_barrier(jnp.sum(route_back.astype(jnp.float32), axis=1)).astype(jnp.bfloat16)
        rows_f = in_rows.astype(jnp.float32)
        part_gate = jnp.einsum('esd,esf->edf', rows_f, gate_grad.astype(jnp.float32))
        part_up = jnp.einsum('esd,esf->edf', rows_f, up_grad.astype(jnp.float32))
        part_down = jnp.einsum('esf,esd->efd', activation.astype(jnp.float32), grad_rows.astype(jnp.float32))
        sum_gate, sum_up, sum_down = carry
        return ((rounded_add(sum_gate, part_gate), rounded_add(sum_up, part_up), rounded_add(sum_down, part_down)), hidden_grad)
    start = (jnp.zeros((EXPERTS, D, FF), jnp.float32), jnp.zeros((EXPERTS, D, FF), jnp.float32), jnp.zeros((EXPERTS, FF, D), jnp.float32))
    sums, hidden_grads = lax.scan(backward_group, start, (hidden_groups, id_groups, grad_groups))
    grad_hidden = hidden_grads.reshape(TOKENS, D)
    return (grad_hidden, grad_route, sums[0], sums[1], sums[2], grad_value)
```

```python
import math

import jax
import jax.numpy as jnp
from jax import lax
from jax.experimental import pallas as pl
from jax.experimental.pallas import tpu as pltpu
from jax.sharding import Mesh, PartitionSpec as P

support_edge = 4.0
smoothing = 0.75
ALL = ("y", "x", "core", "expert")
BF16 = jnp.bfloat16
F32 = jnp.float32
STAT_ROWS = 16
MIB = 1024 * 1024
VMEM_BYTES = 56 * MIB


def dot(left, right, left_dim=1, right_dim=0):
    return lax.dot_general(
        left, right, (((left_dim,), (right_dim,)), ((), ())), preferred_element_type=F32
    )


def params():
    return pltpu.CompilerParams(vmem_limit_bytes=VMEM_BYTES)


def cost(flops, bytes_accessed):
    return pl.CostEstimate(flops=flops, bytes_accessed=bytes_accessed, transcendentals=0)


def whole(shape):
    return pl.BlockSpec(shape, lambda *_: (0,) * len(shape))


def pick(array, index, axis):
    return lax.dynamic_index_in_dim(array, index, axis, keepdims=False)


def swap_cores(array):
    return lax.ppermute(array, "core", [(0, 1), (1, 0)])


def send(arrays, axis_name):
    size = lax.axis_size(axis_name)
    came = {
        shift: lax.ppermute(
            arrays[shift], axis_name, [(k, (k + shift) % size) for k in range(size)]
        )
        for shift in sorted(range(1, size), key=lambda shift: -min(shift, size - shift))
    }
    return [came[shift] for shift in range(1, size)]


def summed(refs):
    total = refs[0][...]
    for ref in refs[1:]:
        total = total + ref[...].astype(F32)
    return total


def slots_kernel(groups, cap, ids_ref, hidden_ref, out_ref, slot_ref, any_ref):
    routes, tok_rows = ids_ref.shape
    ids = ids_ref[...]
    expert = lax.broadcasted_iota(jnp.int32, (8 * pl.cdiv(groups, 8), tok_rows), 0)
    named = [ids[k : k + 1, :] == expert for k in range(routes)]
    counts = sum(jnp.where(n, 1.0, 0.0) for n in named).astype(BF16)
    row = lax.broadcasted_iota(jnp.int32, (tok_rows, tok_rows), 0)
    col = lax.broadcasted_iota(jnp.int32, (tok_rows, tok_rows), 1)
    before = dot(counts, jnp.where(row < col, 1.0, 0.0).astype(BF16))
    slot_ids = lax.broadcasted_iota(jnp.int32, (groups * cap, tok_rows), 0)
    placed = jnp.zeros((groups * cap, tok_rows), F32)
    for k in range(routes):
        position = jnp.sum(jnp.where(named[k], before, 0.0), axis=0, keepdims=True)
        slot = ids[k : k + 1, :] * cap + position.astype(jnp.int32)
        placed = placed + jnp.where(slot_ids == slot, 1.0, 0.0)
        slot_ref[k : k + 1, :] = slot
    placed = placed.astype(BF16)
    any_ref[...] = placed
    width = hidden_ref.shape[1]
    step = min(512, width)
    for at in range(0, width, step):
        out_ref[:, at : at + step] = dot(placed, hidden_ref[:, at : at + step]).astype(BF16)


def front_kernel(
    cap, x_ref, gate_ref, up_ref, mix_ref, stat_ref, *refs
):
    act_ref, one_ref, two_ref, z_ref, acc = refs[-5:]
    step = pl.program_id(0)
    x = x_ref[...]
    gate = dot(x, gate_ref[...])
    up = dot(x, up_ref[...])
    sig = jax.nn.sigmoid(gate)
    act = (gate * sig * up).astype(BF16)
    act_ref[...] = act
    one_ref[...] = up * sig * (1.0 + gate * (1.0 - sig))
    two_ref[...] = gate * sig
    part = dot(act, mix_ref[...])

    @pl.when(step == 0)
    def _():
        acc[...] = part

    @pl.when(step > 0)
    def _():
        acc[...] += part

    @pl.when(step == pl.num_programs(0) - 1)
    def _():
        total = acc[...].astype(BF16)
        shape = (STAT_ROWS, z_ref.shape[2])
        lane = lax.broadcasted_iota(jnp.int32, shape, 1)
        stat = jnp.where(lane < shape[1] // 2, stat_ref[0], stat_ref[1])
        high = stat.astype(BF16).astype(F32)
        middle = (stat - high).astype(BF16).astype(F32)
        low = stat - high - middle
        row = lax.broadcasted_iota(jnp.int32, stat.shape, 0)
        rows = jnp.where(
            row == 0, high, jnp.where(row == 1, middle, jnp.where(row == 2, low, 0.0))
        ).astype(BF16)
        for group in range(z_ref.shape[0]):
            z_ref[group, :cap, :] = total[group * cap : (group + 1) * cap]
            z_ref[group, cap:, :] = rows


def head_kernel(
    cap, token_count, moments_ref, back_ref, slot_ref, weight_ref, resid_ref, returns_ref, *refs
):
    out_ref, grad_ref, route_ref = refs[-3:]
    groups, _, bins = back_ref.shape
    routes, tok_rows = slot_ref.shape
    stat = jnp.sum(jnp.sum(back_ref[:, cap:, :].astype(F32), axis=0), axis=0, keepdims=True)
    half = bins // 2
    batch_mean = stat[:, 0:1] / token_count
    batch_var = stat[:, half : half + 1] / token_count - batch_mean * batch_mean
    run_mean, run_var = moments_ref[0], moments_ref[1]
    mean_value = 0.5 * (run_mean + batch_mean)
    var_value = 0.5 * (run_var + batch_var) + 0.25 * (batch_mean - run_mean) ** 2
    scaled = jnp.clip(
        (returns_ref[...] - mean_value) / jnp.sqrt(var_value + 1e-06), -support_edge, support_edge
    )
    width = 2.0 * support_edge / bins
    scale = math.sqrt(2.0) * smoothing * width
    edge = lax.broadcasted_iota(jnp.int32, (tok_rows, bins), 1).astype(F32) * width - support_edge
    lower = lax.erf((edge - scaled) / scale)
    upper = lax.erf((edge + width - scaled) / scale)
    targets = (upper - lower) / (upper[:, bins - 1 :] - lower[:, :1])

    back = jnp.concatenate([back_ref[group, :cap, :] for group in range(groups)], axis=0)
    slot_ids = lax.broadcasted_iota(jnp.int32, (groups * cap, tok_rows), 0)
    placed, token_logits = [], []
    logits = resid_ref[...]
    for k in range(routes):
        placed.append(jnp.where(slot_ids == slot_ref[k : k + 1, :], 1.0, 0.0).astype(BF16))
        token_logits.append(dot(placed[k], back, 0, 0))
        logits = logits + weight_ref[:, k : k + 1] * token_logits[k]
    power = jnp.exp(logits - jnp.max(logits, axis=1, keepdims=True))
    probs = power / jnp.sum(power, axis=1, keepdims=True)
    grad = (probs - targets).astype(BF16)
    grad_ref[...] = grad
    grad_f = grad.astype(F32)
    total = jnp.zeros((groups * cap, bins), F32)
    which = lax.broadcasted_iota(jnp.int32, (tok_rows, routes), 1)
    route = jnp.zeros((tok_rows, routes), F32)
    for k in range(routes):
        weighted = (weight_ref[:, k : k + 1] * grad_f).astype(BF16)
        total = total + dot(placed[k], weighted)
        sums = jnp.sum(token_logits[k] * grad_f, axis=1, keepdims=True)
        route = jnp.where(which == k, sums, route)
    out_ref[...] = total.astype(BF16)
    route_ref[...] = route


def back_kernel(grad_ref, mix_ref, act_ref, one_ref, two_ref, gate_ref, up_ref, *refs):
    input_ref, pair_ref, inner_ref = refs[-3:]
    ff = one_ref.shape[1]

    @pl.when(pl.program_id(0) == 0)
    def _():
        grad = grad_ref[...]
        act_grad = dot(grad, mix_ref[...], 1, 1)
        pair_ref[:, :ff] = (act_grad * one_ref[...]).astype(BF16)
        pair_ref[:, ff:] = (act_grad * two_ref[...]).astype(BF16)
        inner_ref[...] = dot(act_ref[...], grad, 0, 0).astype(BF16)

    input_ref[...] = (
        dot(pair_ref[:, :ff], gate_ref[...], 1, 1) + dot(pair_ref[:, ff:], up_ref[...], 1, 1)
    ).astype(BF16)


def parts_kernel(
    shifts, coord_ref, rows_x, rows_x2, rows_y, rows_y2, value_x, value_y, resid_x, resid_x2,
    down_x, pair_ref, pair2_ref, inner_ref, inner2_ref, grad_ref, grad2_ref, *refs,
):
    del coord_ref
    outs, inner = refs[:-1], refs[-1]
    step = pl.program_id(0)
    each = len(outs) // (2 * len(shifts))
    ff, bins = inner.shape
    cut = ff - 2 * bins

    @pl.when(step == 0)
    def _():
        inner[...] = (inner_ref[...].astype(F32) + inner2_ref[...].astype(F32)).astype(BF16)

    def flat(ref):
        return ref[...].reshape(ref.shape[0] * ref.shape[1] * ref.shape[2], ref.shape[3])

    def write(place, at, value):
        half = len(outs) // 2
        for number in range(len(shifts)):

            def put():
                targets = outs[place * half + number * each : place * half + (number + 1) * each]
                begin = 0
                for out in targets:
                    low, high = max(at, begin), min(at + value.shape[1], begin + out.shape[2])
                    if low < high:
                        part = value[:, low - at : high - at]
                        out[:, :, low - begin : high - begin] = part.reshape(
                            out.shape[:2] + (high - low,)
                        ).astype(out.dtype)
                    begin += out.shape[2]

            if len(shifts) == 1:
                put()
            else:
                pl.when(step == number)(put)

    write(0, 0, dot(flat(rows_x), pair_ref[:, :ff]) + dot(flat(rows_x2), pair2_ref[:, :ff]))
    write(0, ff, dot(flat(value_x), inner[:cut, :], 1, 1))
    write(
        0,
        ff + cut,
        dot(flat(resid_x), grad_ref[...])
        + dot(flat(resid_x2), grad2_ref[...])
        + dot(flat(down_x), inner[...]),
    )
    write(1, 0, dot(flat(rows_y), pair_ref[:, ff:]) + dot(flat(rows_y2), pair2_ref[:, ff:]))
    write(1, ff, dot(flat(value_y), inner[cut:, :], 1, 1))


def fold_kernel(*refs):
    half = len(refs) // 3
    for number in range(half):
        block, came, out = refs[number], refs[half + number], refs[2 * half + number]
        columns = came.shape[2]
        at = 0 if number % 2 == 0 else columns
        out[:, :, columns - at : 2 * columns - at] = block[:, :, columns - at : 2 * columns - at]
        out[:, :, at : at + columns] = (
            block[:, :, at : at + columns].astype(F32) + came[...].astype(F32)
        ).astype(BF16)


def middle_kernel(side_x, side_y, coord_ref, placed_ref, rows_ref, *refs):
    refs = list(refs)
    firsts = [refs.pop(0) for _ in range(3)]
    seconds = [refs.pop(0) for _ in range(3)]
    hidden_ref, head_ref = refs.pop(0), refs.pop(0)
    first_outs = [refs.pop(0) for _ in range(side_y)]
    second_outs = [refs.pop(0) for _ in range(side_x)]
    first_full, second_full = refs
    columns = first_outs[0].shape[1]
    first_full[...] = summed(firsts)
    second_full[...] = summed(seconds)
    for shift, out in enumerate(first_outs):
        out[...] = first_full[lax.rem(coord_ref[1] + shift, side_y), :, :columns].astype(out.dtype)
    for shift, out in enumerate(second_outs):
        out[...] = second_full[lax.rem(coord_ref[0] + shift, side_x)].astype(out.dtype)
    head_ref[...] = first_full[:, :, columns:]
    hidden_ref[...] = dot(placed_ref[...], rows_ref[...], 0, 0).astype(BF16)


def last_kernel(side_x, side_y, head_ref, *refs):
    firsts, seconds = refs[:side_y], refs[side_y : side_y + side_x]
    gate_ref, up_ref, down_ref, value_ref = refs[side_y + side_x :]
    ff = gate_ref.shape[1]
    first, second = summed(firsts), summed(seconds)
    gate_ref[...] = first[:, :ff]
    up_ref[...] = second[:, :ff]
    cut = first.shape[1] - ff
    down_ref[:, :cut] = first[:, ff:]
    down_ref[:, cut:] = second[:, ff:]
    value_ref[...] = jnp.sum(head_ref[...], axis=0)


def per_shift(count, shape):
    return tuple(jax.ShapeDtypeStruct(shape, BF16 if shift else F32) for shift in range(count))


def per_device(
    hidden_in,
    resid_in,
    route_ids,
    route_weight,
    returns,
    run_moments,
    gate_w,
    up_w,
    down_w,
    value_w,
):
    groups = lax.axis_size("expert")
    side_y, side_x = lax.axis_size("y"), lax.axis_size("x")
    core = lax.axis_index("core")
    tok_rows, width = hidden_in.shape
    routes = route_ids.shape[1]
    cap = 3 * tok_rows * routes // (2 * groups)
    slot_total = groups * cap
    bins = value_w.shape[1]
    gate_w, up_w, down_w = gate_w[0], up_w[0], down_w[0]
    ff = gate_w.shape[1]
    own_rows = width // (side_y * side_x * 2)
    token_count = float(tok_rows * groups * side_y * side_x * 2)
    sds = jax.ShapeDtypeStruct
    anywhere = pl.BlockSpec(memory_space=pl.ANY)
    smem = pl.BlockSpec(memory_space=pltpu.SMEM)
    vmem = pl.BlockSpec(memory_space=pltpu.VMEM)

    def core_half(array):
        blocks = array.reshape(side_y * side_x, 2, own_rows, array.shape[1])
        mine = pick(blocks, core, 1).reshape(width // 2, array.shape[1])
        other = pick(blocks, 1 - core, 1).reshape(width // 2, array.shape[1])
        return mine, other

    def exchange(blocks):
        return lax.all_to_all(blocks, "expert", 0, 0, tiled=True)

    def exchange_rows(rows):
        return exchange(rows.reshape(groups, cap, rows.shape[1])).reshape(rows.shape)

    outgoing, slots, placed_any = pl.pallas_call(
        lambda *refs: slots_kernel(groups, cap, *refs),
        out_shape=(
            sds((slot_total, width), BF16),
            sds((routes, tok_rows), jnp.int32),
            sds((slot_total, tok_rows), BF16),
        ),
        compiler_params=params(),
        cost_estimate=cost(2 * tok_rows * slot_total * width, 2 * width * (slot_total + tok_rows)),
        name="slots",
    )(route_ids.T, hidden_in)
    in_rows = exchange_rows(outgoing)

    with jax.named_scope("moments"):
        sums = jnp.stack([jnp.sum(returns), jnp.sum(returns * returns)])
        for axis_name in ("x", "y", "core"):
            sums = lax.psum(sums, axis_name)

    with jax.named_scope("weights_only"):
        mix = dot(down_w, value_w).astype(BF16)
        resid_logits = dot(resid_in, value_w)
        value_mine, _ = core_half(value_w)
        down_mine, _ = core_half(down_w.T)
        resid_mine, resid_other = core_half(resid_in.T)
        resid_peer = swap_cores(resid_other)

    steps = 3
    part = ff // steps
    act, one, two, route_logits = pl.pallas_call(
        lambda *refs: front_kernel(cap, *refs),
        grid=(steps,),
        in_specs=[
            whole((slot_total, width)),
            pl.BlockSpec((width, part), lambda j: (0, j)),
            pl.BlockSpec((width, part), lambda j: (0, j)),
            pl.BlockSpec((part, bins), lambda j: (j, 0)),
            smem,
        ]
        + [anywhere] * 4,
        out_specs=[
            pl.BlockSpec((slot_total, part), lambda j: (0, j)),
            pl.BlockSpec((slot_total, part), lambda j: (0, j)),
            pl.BlockSpec((slot_total, part), lambda j: (0, j)),
            whole((groups, cap + STAT_ROWS, bins)),
        ],
        out_shape=(
            sds((slot_total, ff), BF16),
            sds((slot_total, ff), F32),
            sds((slot_total, ff), F32),
            sds((groups, cap + STAT_ROWS, bins), BF16),
        ),
        scratch_shapes=[pltpu.VMEM((slot_total, bins), F32)],
        compiler_params=params(),
        cost_estimate=cost(4 * slot_total * width * ff, 4 * width * ff),
        name="front",
    )(in_rows, gate_w, up_w, mix, sums, value_mine, down_mine, resid_mine, resid_peer)
    back_logits = exchange(route_logits)
    with jax.named_scope("turned"):
        rows_mine, rows_other = core_half(in_rows.T)
        rows_peer = swap_cores(rows_other)

    out_grad, logit_grad, grad_route = pl.pallas_call(
        lambda *refs: head_kernel(cap, token_count, *refs),
        in_specs=[smem]
        + [vmem] * 5
        + [anywhere] * 2,
        out_shape=(
            sds((slot_total, bins), BF16),
            sds((tok_rows, bins), BF16),
            sds((tok_rows, routes), F32),
        ),
        compiler_params=params(),
        cost_estimate=cost(8 * tok_rows * slot_total * bins, 4 * slot_total * bins),
        name="head",
    )(
        run_moments, back_logits, slots, route_weight, resid_logits, returns.reshape(tok_rows, 1),
        rows_mine, rows_other,
    )
    row_grad = exchange_rows(out_grad)
    grad_peer = swap_cores(logit_grad)

    strip = min(512, width)
    input_grad, pair, inner = pl.pallas_call(
        back_kernel,
        grid=(width // strip,),
        in_specs=[
            whole((slot_total, bins)),
            whole((ff, bins)),
            whole((slot_total, ff)),
            whole((slot_total, ff)),
            whole((slot_total, ff)),
            pl.BlockSpec((strip, ff), lambda i: (i, 0)),
            pl.BlockSpec((strip, ff), lambda i: (i, 0)),
            anywhere,
            anywhere,
        ],
        out_specs=[
            pl.BlockSpec((slot_total, strip), lambda i: (0, i)),
            whole((slot_total, 2 * ff)),
            whole((ff, bins)),
        ],
        out_shape=(
            sds((slot_total, width), BF16),
            sds((slot_total, 2 * ff), BF16),
            sds((ff, bins), BF16),
        ),
        compiler_params=params(),
        cost_estimate=cost(4 * slot_total * width * ff, 4 * width * ff),
        name="back",
    )(row_grad, mix, act, one, two, gate_w, up_w, rows_peer, grad_peer)
    back_grad = exchange_rows(input_grad)
    inner_peer = swap_cores(inner)
    pair_peer = swap_cores(pair)

    half = width // 2
    coords = jnp.stack([lax.axis_index("x"), lax.axis_index("y")]).astype(jnp.int32)
    def parts(shifts, out_shape):
        pattern = {(2,): lambda step: 2, (1, 3, 0): lambda step: lax.rem(2 * step + 1, 5)}[shifts]

        def tall(depth):
            return pl.BlockSpec(
                (side_y, 1, own_rows, depth),
                lambda step, at: (0, lax.rem(at[0] + pattern(step), side_x), 0, 0),
            )

        def wide(depth):
            return pl.BlockSpec(
                (1, side_x, own_rows, depth),
                lambda step, at: (lax.rem(at[1] + pattern(step), side_y), 0, 0, 0),
            )

        return pl.pallas_call(
            lambda *refs: parts_kernel(shifts, *refs),
            grid_spec=pltpu.PrefetchScalarGridSpec(
                num_scalar_prefetch=1,
                grid=(len(shifts),),
                in_specs=[
                    tall(slot_total),
                    tall(slot_total),
                    wide(slot_total),
                    wide(slot_total),
                    tall(bins),
                    wide(bins),
                    tall(tok_rows),
                    tall(tok_rows),
                    tall(ff),
                    whole((slot_total, 2 * ff)),
                    whole((slot_total, 2 * ff)),
                    whole((ff, bins)),
                    whole((ff, bins)),
                    whole((tok_rows, bins)),
                    whole((tok_rows, bins)),
                ],
                out_specs=[whole(out.shape) for out in out_shape],
                scratch_shapes=[pltpu.VMEM((ff, bins), BF16)],
            ),
            out_shape=out_shape,
            compiler_params=params(),
            cost_estimate=cost(len(shifts) * half * slot_total * 2 * ff, len(shifts) * 4 * MIB),
            name="parts%d" % len(shifts),
        )(
            coords,
            *[
                rows.reshape(side_y, side_x, own_rows, rows.shape[1])
                for rows in (
                    rows_mine, rows_peer, rows_mine, rows_peer, value_mine, value_mine, resid_mine,
                    resid_peer, down_mine,
                )
            ],
            pair,
            pair_peer,
            inner,
            inner_peer,
            logit_grad,
            grad_peer,
        )

    def step_on(array, axis_name, shift):
        size = lax.axis_size(axis_name)
        return lax.ppermute(array, axis_name, [(k, (k + shift) % size) for k in range(size)])

    cut = ff - 2 * bins
    first_columns, second_columns = ff + cut, 2 * ff - cut
    columns = first_columns + bins
    block = (side_y, own_rows, columns)
    far = sds((side_y, own_rows, columns // 2), BF16)
    x_up, x_down, y_up, y_down = parts((2,), (far,) * 4)
    came = (
        step_on(x_up, "x", 1),
        step_on(x_down, "x", -1),
        step_on(y_up, "y", 1),
        step_on(y_down, "y", -1),
    )
    near, own = sds(block, BF16), sds(block, F32)
    x_up, x_down, x_own, y_up, y_down, y_own = parts(
        (1, 3, 0), (near, near, own, near, near, own)
    )
    x_up, x_down, y_up, y_down = pl.pallas_call(
        fold_kernel,
        out_shape=(near,) * 4,
        compiler_params=params(),
        cost_estimate=cost(0, 24 * side_y * own_rows * columns),
        name="fold",
    )(x_up, x_down, y_up, y_down, *came)
    firsts = (x_own, step_on(x_up, "x", 1), step_on(x_down, "x", -1))
    seconds = (y_own, step_on(y_up, "y", 1), step_on(y_down, "y", -1))

    grad_hidden, head, *halves = pl.pallas_call(
        lambda *refs: middle_kernel(side_x, side_y, *refs),
        in_specs=[smem] + [vmem] * 8,
        out_shape=(
            sds((tok_rows, width), BF16),
            sds((side_y, own_rows, bins), F32),
        )
        + per_shift(side_y, (own_rows, first_columns))
        + per_shift(side_x, (own_rows, second_columns)),
        scratch_shapes=[pltpu.VMEM(block, F32), pltpu.VMEM(block, F32)],
        compiler_params=params(),
        cost_estimate=cost(2 * tok_rows * slot_total * width, 2 * width * (slot_total + tok_rows)),
        name="middle",
    )(coords, placed_any, back_grad, *firsts, *seconds)
    firsts, seconds = halves[:side_y], halves[side_y:]
    shares = head.reshape(side_y * groups, own_rows // groups, bins)
    shares = lax.all_to_all(shares, ("y", "expert"), 0, 0, tiled=True)
    first_came, second_came = send(firsts, "y"), send(seconds, "x")
    grad_gate, grad_up, grad_down, grad_value = pl.pallas_call(
        lambda *refs: last_kernel(side_x, side_y, *refs),
        out_shape=(
            sds((own_rows, ff), F32),
            sds((own_rows, ff), F32),
            sds((own_rows, ff), F32),
            sds(shares.shape[1:], F32),
        ),
        compiler_params=params(),
        cost_estimate=cost(0, 24 * own_rows * ff),
        name="last",
    )(shares, firsts[0], *first_came, seconds[0], *second_came)
    return (grad_hidden, grad_route, grad_gate[None], grad_up[None], grad_down.T[None], grad_value)


def solution(mesh):
    pair = 2
    plane = mesh.shape["dp"] // pair
    side = math.isqrt(plane)
    grid = Mesh(mesh.devices.reshape(plane // side, side, pair, mesh.shape["expert"]), ALL)
    rows = P(ALL, None)
    dp = ("y", "x", "core")
    in_specs = (
        rows,
        rows,
        rows,
        rows,
        P(ALL),
        P(),
        P("expert", None, None),
        P("expert", None, None),
        P("expert", None, None),
        P(),
    )
    out_specs = (
        rows,
        rows,
        P("expert", dp, None),
        P("expert", dp, None),
        P("expert", None, dp),
        rows,
    )
    return jax.shard_map(
        per_device, mesh=grid, in_specs=in_specs, out_specs=out_specs, check_vma=False
    )
```

```python
import math

import jax
import jax.numpy as jnp
from jax import lax
from jax.experimental import pallas as pl
from jax.experimental.pallas import tpu as pltpu
from jax.sharding import Mesh, PartitionSpec as P

support_edge = 4.0
smoothing = 0.75
ALL = ("y", "x", "core", "expert")
BF16 = jnp.bfloat16
F32 = jnp.float32
STAT_ROWS = 16
MIB = 1024 * 1024
VMEM_BYTES = 56 * MIB


def dot(left, right, left_dim=1, right_dim=0):
    return lax.dot_general(
        left, right, (((left_dim,), (right_dim,)), ((), ())), preferred_element_type=F32
    )


def params():
    return pltpu.CompilerParams(vmem_limit_bytes=VMEM_BYTES)


def cost(flops, bytes_accessed):
    return pl.CostEstimate(flops=flops, bytes_accessed=bytes_accessed, transcendentals=0)


def whole(shape):
    return pl.BlockSpec(shape, lambda *_: (0,) * len(shape))


def pick(array, index, axis):
    return lax.dynamic_index_in_dim(array, index, axis, keepdims=False)


def swap_cores(array):
    return lax.ppermute(array, "core", [(0, 1), (1, 0)])


def send(arrays, axis_name):
    size = lax.axis_size(axis_name)
    came = {
        shift: lax.ppermute(
            arrays[shift], axis_name, [(k, (k + shift) % size) for k in range(size)]
        )
        for shift in sorted(range(1, size), key=lambda shift: -min(shift, size - shift))
    }
    return [came[shift] for shift in range(1, size)]


def summed(refs):
    total = refs[0][...].astype(F32)
    for ref in refs[1:]:
        total = total + ref[...].astype(F32)
    return total


def slots_kernel(groups, cap, ids_ref, hidden_ref, out_ref, slot_ref, any_ref):
    routes, tok_rows = ids_ref.shape
    ids = ids_ref[...]
    expert = lax.broadcasted_iota(jnp.int32, (8 * pl.cdiv(groups, 8), tok_rows), 0)
    named = [ids[k : k + 1, :] == expert for k in range(routes)]
    counts = sum(jnp.where(n, 1.0, 0.0) for n in named).astype(BF16)
    row = lax.broadcasted_iota(jnp.int32, (tok_rows, tok_rows), 0)
    col = lax.broadcasted_iota(jnp.int32, (tok_rows, tok_rows), 1)
    before = dot(counts, jnp.where(row < col, 1.0, 0.0).astype(BF16))
    slot_ids = lax.broadcasted_iota(jnp.int32, (groups * cap, tok_rows), 0)
    placed = jnp.zeros((groups * cap, tok_rows), F32)
    for k in range(routes):
        position = jnp.sum(jnp.where(named[k], before, 0.0), axis=0, keepdims=True)
        slot = ids[k : k + 1, :] * cap + position.astype(jnp.int32)
        placed = placed + jnp.where(slot_ids == slot, 1.0, 0.0)
        slot_ref[k : k + 1, :] = slot
    placed = placed.astype(BF16)
    any_ref[...] = placed
    width = hidden_ref.shape[1]
    step = min(512, width)
    for at in range(0, width, step):
        out_ref[:, at : at + step] = dot(placed, hidden_ref[:, at : at + step]).astype(BF16)


def front_kernel(
    cap, x_ref, gate_ref, up_ref, mix_ref, stat_ref, *refs
):
    act_ref, one_ref, two_ref, z_ref, acc = refs[-5:]
    step = pl.program_id(0)
    x = x_ref[...]
    gate = dot(x, gate_ref[...])
    up = dot(x, up_ref[...])
    sig = jax.nn.sigmoid(gate)
    act = (gate * sig * up).astype(BF16)
    act_ref[...] = act
    one_ref[...] = up * sig * (1.0 + gate * (1.0 - sig))
    two_ref[...] = gate * sig
    part = dot(act, mix_ref[...])

    @pl.when(step == 0)
    def _():
        acc[...] = part

    @pl.when(step > 0)
    def _():
        acc[...] += part

    @pl.when(step == pl.num_programs(0) - 1)
    def _():
        total = acc[...].astype(BF16)
        shape = (STAT_ROWS, z_ref.shape[2])
        lane = lax.broadcasted_iota(jnp.int32, shape, 1)
        stat = jnp.where(lane < shape[1] // 2, stat_ref[0], stat_ref[1])
        high = stat.astype(BF16).astype(F32)
        middle = (stat - high).astype(BF16).astype(F32)
        low = stat - high - middle
        row = lax.broadcasted_iota(jnp.int32, stat.shape, 0)
        rows = jnp.where(
            row == 0, high, jnp.where(row == 1, middle, jnp.where(row == 2, low, 0.0))
        ).astype(BF16)
        for group in range(z_ref.shape[0]):
            z_ref[group, :cap, :] = total[group * cap : (group + 1) * cap]
            z_ref[group, cap:, :] = rows


def head_kernel(
    cap, token_count, moments_ref, back_ref, slot_ref, weight_ref, resid_ref, returns_ref, *refs
):
    out_ref, grad_ref, route_ref = refs[-3:]
    groups, _, bins = back_ref.shape
    routes, tok_rows = slot_ref.shape
    stat = jnp.sum(jnp.sum(back_ref[:, cap:, :].astype(F32), axis=0), axis=0, keepdims=True)
    half = bins // 2
    batch_mean = stat[:, 0:1] / token_count
    batch_var = stat[:, half : half + 1] / token_count - batch_mean * batch_mean
    run_mean, run_var = moments_ref[0], moments_ref[1]
    mean_value = 0.5 * (run_mean + batch_mean)
    var_value = 0.5 * (run_var + batch_var) + 0.25 * (batch_mean - run_mean) ** 2
    scaled = jnp.clip(
        (returns_ref[...] - mean_value) / jnp.sqrt(var_value + 1e-06), -support_edge, support_edge
    )
    width = 2.0 * support_edge / bins
    scale = math.sqrt(2.0) * smoothing * width
    edge = lax.broadcasted_iota(jnp.int32, (tok_rows, bins), 1).astype(F32) * width - support_edge
    lower = lax.erf((edge - scaled) / scale)
    upper = lax.erf((edge + width - scaled) / scale)
    targets = (upper - lower) / (upper[:, bins - 1 :] - lower[:, :1])

    back = jnp.concatenate([back_ref[group, :cap, :] for group in range(groups)], axis=0)
    slot_ids = lax.broadcasted_iota(jnp.int32, (groups * cap, tok_rows), 0)
    placed, token_logits = [], []
    logits = resid_ref[...]
    for k in range(routes):
        placed.append(jnp.where(slot_ids == slot_ref[k : k + 1, :], 1.0, 0.0).astype(BF16))
        token_logits.append(dot(placed[k], back, 0, 0))
        logits = logits + weight_ref[:, k : k + 1] * token_logits[k]
    power = jnp.exp(logits - jnp.max(logits, axis=1, keepdims=True))
    probs = power / jnp.sum(power, axis=1, keepdims=True)
    grad = (probs - targets).astype(BF16)
    grad_ref[...] = grad
    grad_f = grad.astype(F32)
    total = jnp.zeros((groups * cap, bins), F32)
    which = lax.broadcasted_iota(jnp.int32, (tok_rows, routes), 1)
    route = jnp.zeros((tok_rows, routes), F32)
    for k in range(routes):
        weighted = (weight_ref[:, k : k + 1] * grad_f).astype(BF16)
        total = total + dot(placed[k], weighted)
        sums = jnp.sum(token_logits[k] * grad_f, axis=1, keepdims=True)
        route = jnp.where(which == k, sums, route)
    out_ref[...] = total.astype(BF16)
    route_ref[...] = route


def back_kernel(grad_ref, mix_ref, one_ref, two_ref, gate_ref, up_ref, *refs):
    input_ref, pair_ref = refs[-2:]
    ff = one_ref.shape[1]

    @pl.when(pl.program_id(0) == 0)
    def _():
        act_grad = dot(grad_ref[...], mix_ref[...], 1, 1)
        pair_ref[:, :ff] = (act_grad * one_ref[...]).astype(BF16)
        pair_ref[:, ff:] = (act_grad * two_ref[...]).astype(BF16)

    input_ref[...] = (
        dot(pair_ref[:, :ff], gate_ref[...], 1, 1) + dot(pair_ref[:, ff:], up_ref[...], 1, 1)
    ).astype(BF16)


def far_kernel(
    coord_ref, rows_x, rows_x2, resid_x, resid_x2, down_x, rows_y, rows_y2, value_y, pair_ref,
    grad_ref, grad2_ref, row_grad, row_grad2, mix_ref, one2_ref, two2_ref, act_ref, act2_ref,
    first_ref, second_ref, pair2_ref, inner_ref,
):
    ff = act_ref.shape[1]
    act_grad = dot(row_grad2[...], mix_ref[...], 1, 1)
    pair2_ref[:, :ff] = (act_grad * one2_ref[...]).astype(BF16)
    pair2_ref[:, ff:] = (act_grad * two2_ref[...]).astype(BF16)
    inner_ref[...] = (
        dot(act_ref[...], row_grad[...], 0, 0) + dot(act2_ref[...], row_grad2[...], 0, 0)
    ).astype(BF16)
    gates, ups = slice(None, ff), slice(ff, None)
    x_kernel(
        1, coord_ref, rows_x, rows_x2, resid_x, resid_x2, down_x, pair_ref.at[:, gates],
        pair2_ref.at[:, gates], inner_ref, grad_ref, grad2_ref, first_ref,
    )
    y_kernel(
        1, coord_ref, rows_y, rows_y2, value_y, pair_ref.at[:, ups], pair2_ref.at[:, ups],
        inner_ref, second_ref,
    )


def own_kernel(
    coord_ref, rows_x, rows_x2, resid_x, resid_x2, down_x, rows_y, rows_y2, value_y, pair_ref,
    pair2_ref, inner_ref, grad_ref, grad2_ref, token, first_ref, second_ref,
):
    del token
    ff = inner_ref.shape[0]
    gates, ups = slice(None, ff), slice(ff, None)
    x_kernel(
        1, coord_ref, rows_x, rows_x2, resid_x, resid_x2, down_x, pair_ref.at[:, gates],
        pair2_ref.at[:, gates], inner_ref, grad_ref, grad2_ref, first_ref,
    )
    y_kernel(
        1, coord_ref, rows_y, rows_y2, value_y, pair_ref.at[:, ups], pair2_ref.at[:, ups],
        inner_ref, second_ref,
    )


def flat(ref):
    return ref[...].reshape(ref.shape[0] * ref.shape[1] * ref.shape[2], ref.shape[3])


def write(outs, at, value):
    for number, out in enumerate(outs):

        def put():
            shape = out.shape[:2] + (value.shape[1],)
            out[:, :, at : at + value.shape[1]] = value.reshape(shape).astype(out.dtype)

        if len(outs) == 1:
            put()
        else:
            pl.when(pl.program_id(0) == number)(put)


def x_kernel(
    count, coord_ref, rows_x, rows_x2, resid_x, resid_x2, down_x, pair_ref, pair2_ref, inner_ref,
    grad_ref, grad2_ref, *outs,
):
    del coord_ref
    outs = outs[-count:]
    write(outs, 0, dot(flat(rows_x), pair_ref[...]) + dot(flat(rows_x2), pair2_ref[...]))
    write(
        outs,
        pair_ref.shape[1],
        dot(flat(resid_x), grad_ref[...])
        + dot(flat(resid_x2), grad2_ref[...])
        + dot(flat(down_x), inner_ref[...]),
    )


def y_kernel(
    count, coord_ref, rows_y, rows_y2, value_y, pair_ref, pair2_ref, inner_ref, *outs
):
    del coord_ref
    outs = outs[-count:]
    write(outs, 0, dot(flat(rows_y), pair_ref[...]) + dot(flat(rows_y2), pair2_ref[...]))
    write(outs, pair_ref.shape[1], dot(flat(value_y), inner_ref[...], 1, 1))


def first_kernel(coord_ref, *refs):
    full, head_ref, outs = refs[-1], refs[-6], refs[-5:-1]
    columns = outs[0].shape[1]
    full[...] = summed(refs[:4])
    head_ref[...] = full[:, :, columns:]
    for shift, out in enumerate(outs):
        at = lax.rem(coord_ref[1] + shift, full.shape[0])
        out[...] = full[at, :, :columns].astype(out.dtype)


def second_kernel(coord_ref, *refs):
    full, outs = refs[-1], refs[-5:-1]
    full[...] = summed(refs[:4])
    for shift, out in enumerate(outs):
        out[...] = full[lax.rem(coord_ref[0] + shift, full.shape[0])].astype(out.dtype)


def hidden_kernel(placed_ref, rows_ref, head_ref, out_ref, pass_ref):
    out_ref[...] = dot(placed_ref[...], rows_ref[...], 0, 0).astype(BF16)
    pass_ref[...] = head_ref[...]


def last_kernel(side_x, side_y, head_ref, *refs):
    firsts, seconds = refs[:side_y], refs[side_y : side_y + side_x]
    gate_ref, up_ref, down_ref, value_ref = refs[side_y + side_x :]
    ff = gate_ref.shape[1]
    gate_ref[...] = summed(firsts)
    second = summed(seconds)
    up_ref[...] = second[:, :ff]
    down_ref[...] = second[:, ff:]
    value_ref[...] = jnp.sum(head_ref[...], axis=0)


def turn_kernel(core_ref, rows_ref, token, mine_ref, other_ref):
    del token
    own = mine_ref.shape[1]
    for at in range(mine_ref.shape[0]):
        turned = rows_ref[:, 2 * own * at : 2 * own * (at + 1)].T
        low, high = turned[:own], turned[own:]
        mine_ref[at] = jnp.where(core_ref[0] == 0, low, high)
        other_ref[at] = jnp.where(core_ref[0] == 0, high, low)


def per_shift(count, shape):
    return tuple(jax.ShapeDtypeStruct(shape, BF16 if shift else F32) for shift in range(count))


def per_device(
    hidden_in,
    resid_in,
    route_ids,
    route_weight,
    returns,
    run_moments,
    gate_w,
    up_w,
    down_w,
    value_w,
):
    groups = lax.axis_size("expert")
    side_y, side_x = lax.axis_size("y"), lax.axis_size("x")
    core = lax.axis_index("core")
    tok_rows, width = hidden_in.shape
    routes = route_ids.shape[1]
    cap = 3 * tok_rows * routes // (2 * groups)
    slot_total = groups * cap
    bins = value_w.shape[1]
    gate_w, up_w, down_w = gate_w[0], up_w[0], down_w[0]
    ff = gate_w.shape[1]
    own_rows = width // (side_y * side_x * 2)
    token_count = float(tok_rows * groups * side_y * side_x * 2)
    sds = jax.ShapeDtypeStruct
    anywhere = pl.BlockSpec(memory_space=pl.ANY)
    smem = pl.BlockSpec(memory_space=pltpu.SMEM)
    vmem = pl.BlockSpec(memory_space=pltpu.VMEM)

    coords = jnp.stack([lax.axis_index("x"), lax.axis_index("y")]).astype(jnp.int32)

    def core_half(array):
        blocks = array.reshape(side_y * side_x, 2, own_rows, array.shape[1])
        mine = pick(blocks, core, 1).reshape(width // 2, array.shape[1])
        other = pick(blocks, 1 - core, 1).reshape(width // 2, array.shape[1])
        return mine, other

    def exchange(blocks):
        return lax.all_to_all(blocks, "expert", 0, 0, tiled=True)

    def exchange_rows(rows):
        return exchange(rows.reshape(groups, cap, rows.shape[1])).reshape(rows.shape)

    outgoing, slots, placed_any = pl.pallas_call(
        lambda *refs: slots_kernel(groups, cap, *refs),
        out_shape=(
            sds((slot_total, width), BF16),
            sds((routes, tok_rows), jnp.int32),
            sds((slot_total, tok_rows), BF16),
        ),
        compiler_params=params(),
        cost_estimate=cost(2 * tok_rows * slot_total * width, 2 * width * (slot_total + tok_rows)),
        name="slots",
    )(route_ids.T, hidden_in)
    in_rows = exchange_rows(outgoing)

    with jax.named_scope("moments"):
        sums = jnp.stack([jnp.sum(returns), jnp.sum(returns * returns)])
        for axis_name in ("x", "y", "core"):
            sums = lax.psum(sums, axis_name)

    with jax.named_scope("weights_only"):
        mix = dot(down_w, value_w).astype(BF16)
        resid_logits = dot(resid_in, value_w)
        value_mine, _ = core_half(value_w)
        down_mine, _ = core_half(down_w.T)
        resid_mine, resid_other = core_half(resid_in.T)
        resid_peer = swap_cores(resid_other)

    steps = 1
    part = ff // steps
    act, one, two, route_logits = pl.pallas_call(
        lambda *refs: front_kernel(cap, *refs),
        grid=(steps,),
        in_specs=[
            whole((slot_total, width)),
            pl.BlockSpec((width, part), lambda j: (0, j)),
            pl.BlockSpec((width, part), lambda j: (0, j)),
            pl.BlockSpec((part, bins), lambda j: (j, 0)),
            smem,
        ]
        + [anywhere] * 4,
        out_specs=[
            pl.BlockSpec((slot_total, part), lambda j: (0, j)),
            pl.BlockSpec((slot_total, part), lambda j: (0, j)),
            pl.BlockSpec((slot_total, part), lambda j: (0, j)),
            whole((groups, cap + STAT_ROWS, bins)),
        ],
        out_shape=(
            sds((slot_total, ff), BF16),
            sds((slot_total, ff), F32),
            sds((slot_total, ff), F32),
            sds((groups, cap + STAT_ROWS, bins), BF16),
        ),
        scratch_shapes=[pltpu.VMEM((slot_total, bins), F32)],
        compiler_params=params(),
        cost_estimate=cost(4 * slot_total * width * ff, 4 * width * ff),
        name="front",
    )(in_rows, gate_w, up_w, mix, sums, value_mine, down_mine, resid_mine, resid_peer)
    back_logits = exchange(route_logits)
    with jax.named_scope("turned"):
        chips = side_y * side_x
        rows_mine, rows_other = pl.pallas_call(
            turn_kernel,
            grid=(4,),
            in_specs=[
                smem,
                pl.BlockSpec((slot_total, width // 4), lambda i: (0, i)),
                anywhere,
            ],
            out_specs=[pl.BlockSpec((chips // 4, own_rows, slot_total), lambda i: (i, 0, 0))] * 2,
            out_shape=(sds((chips, own_rows, slot_total), BF16),) * 2,
            compiler_params=params(),
            cost_estimate=cost(0, 4 * slot_total * width),
            name="turn",
        )(core.astype(jnp.int32)[None], in_rows, act)
        rows_mine = rows_mine.reshape(width // 2, slot_total)
        rows_peer = swap_cores(rows_other).reshape(width // 2, slot_total)
        act_peer, one_peer, two_peer = swap_cores(act), swap_cores(one), swap_cores(two)

    out_grad, logit_grad, grad_route = pl.pallas_call(
        lambda *refs: head_kernel(cap, token_count, *refs),
        in_specs=[smem]
        + [vmem] * 5
        + [anywhere] * 2
        + [smem],
        out_shape=(
            sds((slot_total, bins), BF16),
            sds((tok_rows, bins), BF16),
            sds((tok_rows, routes), F32),
        ),
        compiler_params=params(),
        cost_estimate=cost(8 * tok_rows * slot_total * bins, 4 * slot_total * bins),
        name="head",
    )(
        run_moments, back_logits, slots, route_weight, resid_logits, returns.reshape(tok_rows, 1),
        rows_mine, rows_other, coords,
    )
    row_grad = exchange_rows(out_grad)
    grad_peer = swap_cores(logit_grad)

    row_grad_peer = swap_cores(row_grad)

    strip = min(1024, width)
    input_grad, pair = pl.pallas_call(
        back_kernel,
        grid=(width // strip,),
        in_specs=[
            whole((slot_total, bins)),
            whole((ff, bins)),
            whole((slot_total, ff)),
            whole((slot_total, ff)),
            pl.BlockSpec((strip, ff), lambda i: (i, 0)),
            pl.BlockSpec((strip, ff), lambda i: (i, 0)),
        ]
        + [anywhere] * 5,
        out_specs=[
            pl.BlockSpec((slot_total, strip), lambda i: (0, i)),
            whole((slot_total, 2 * ff)),
        ],
        out_shape=(
            sds((slot_total, width), BF16),
            sds((slot_total, 2 * ff), BF16),
        ),
        compiler_params=params(),
        cost_estimate=cost(4 * slot_total * width * ff, 4 * width * ff),
        name="back",
    )(
        row_grad, mix, one, two, gate_w, up_w, rows_peer, grad_peer, act_peer, one_peer, two_peer
    )
    back_grad = exchange_rows(input_grad)

    half = width // 2
    first_block, second_block = (side_y, own_rows, ff + bins), (side_x, own_rows, 2 * ff)

    def parts(kernel, shifts, blocked, shared, outs, name):
        def shift_of(step):
            return shifts[0] if len(shifts) == 1 else shifts[0] + step * (shifts[1] - shifts[0])

        def tall(depth):
            return pl.BlockSpec(
                (side_y, 1, own_rows, depth),
                lambda step, at: (0, lax.rem(at[0] + shift_of(step), side_x), 0, 0),
            )

        def wide(depth):
            return pl.BlockSpec(
                (1, side_x, own_rows, depth),
                lambda step, at: (lax.rem(at[1] + shift_of(step), side_y), 0, 0, 0),
            )

        makes = {"x": tall, "y": wide}
        return pl.pallas_call(
            kernel,
            grid_spec=pltpu.PrefetchScalarGridSpec(
                num_scalar_prefetch=1,
                grid=(len(shifts),),
                in_specs=[makes[along](rows.shape[1]) for along, rows in blocked]
                + [whole(item.shape) if spec is None else spec for spec, item in shared],
                out_specs=[whole(out.shape) for out in outs],
            ),
            out_shape=outs,
            compiler_params=params(),
            cost_estimate=cost(len(shifts) * half * slot_total * ff, len(shifts) * 3 * MIB),
            name=name,
        )(
            coords,
            *[rows.reshape(side_y, side_x, own_rows, rows.shape[1]) for _, rows in blocked],
            *[item for _, item in shared],
        )

    def step_on(array, axis_name, shift):
        size = lax.axis_size(axis_name)
        return lax.ppermute(array, axis_name, [(k, (k + shift) % size) for k in range(size)])

    x_rows = [("x", r) for r in (rows_mine, rows_peer, resid_mine, resid_peer, down_mine)]
    y_rows = [("y", r) for r in (rows_mine, rows_peer, value_mine)]
    first_out, second_out = sds(first_block, BF16), sds(second_block, BF16)
    first_far, second_far, pair_peer, inner = parts(
        far_kernel,
        (2,),
        x_rows + y_rows,
        [
            (None, item)
            for item in (
                pair, logit_grad, grad_peer, row_grad, row_grad_peer, mix, one_peer, two_peer,
                act, act_peer,
            )
        ],
        [first_out, second_out, sds(pair.shape, BF16), sds((ff, bins), BF16)],
        "far",
    )
    gate_spec = pl.BlockSpec((slot_total, ff), lambda *_: (0, 0))
    up_spec = pl.BlockSpec((slot_total, ff), lambda *_: (0, 1))

    firsts = [step_on(first_far, "x", 2)]
    seconds = [step_on(second_far, "y", 2)]
    first_up, first_down = parts(
        lambda *refs: x_kernel(2, *refs),
        (1, 3),
        x_rows,
        [
            (gate_spec, pair), (gate_spec, pair_peer), (None, inner), (None, logit_grad),
            (None, grad_peer),
        ],
        [first_out] * 2,
        "x_near",
    )
    firsts += [step_on(first_up, "x", 1), step_on(first_down, "x", 3)]
    first_own, second_own = parts(
        own_kernel,
        (0,),
        x_rows + y_rows,
        [
            (None, pair), (None, pair_peer), (None, inner), (None, logit_grad), (None, grad_peer),
            (anywhere, first_up),
        ],
        [first_out, second_out],
        "own",
    )
    second_up, second_down = parts(
        lambda *refs: y_kernel(2, *refs),
        (1, 3),
        y_rows,
        [
            (up_spec, pair), (up_spec, pair_peer), (None, inner), (anywhere, seconds[0]),
            (anywhere, second_own),
        ],
        [second_out] * 2,
        "y_near",
    )
    seconds += [step_on(second_up, "y", 1), step_on(second_down, "y", 3)]

    head, *firsts = pl.pallas_call(
        first_kernel,
        in_specs=[smem] + [vmem] * 4,
        out_shape=(sds((side_y, own_rows, bins), F32),) + per_shift(side_y, (own_rows, ff)),
        scratch_shapes=[pltpu.VMEM(first_block, F32)],
        compiler_params=params(),
        cost_estimate=cost(0, 12 * side_y * own_rows * ff),
        name="first",
    )(coords, first_own, *firsts)
    first_came = send(firsts, "y")
    seconds = pl.pallas_call(
        second_kernel,
        in_specs=[smem] + [vmem] * 4,
        out_shape=per_shift(side_x, (own_rows, 2 * ff)),
        scratch_shapes=[pltpu.VMEM(second_block, F32)],
        compiler_params=params(),
        cost_estimate=cost(0, 24 * side_y * own_rows * ff),
        name="second",
    )(coords, second_own, *seconds)
    second_came = send(seconds, "x")
    grad_hidden, head = pl.pallas_call(
        hidden_kernel,
        out_shape=(sds((tok_rows, width), BF16), sds(head.shape, F32)),
        compiler_params=params(),
        cost_estimate=cost(2 * tok_rows * slot_total * width, 2 * width * (slot_total + tok_rows)),
        name="hidden",
    )(placed_any, back_grad, head)
    shares = head.reshape(side_y * groups, own_rows // groups, bins)
    shares = lax.all_to_all(shares, ("y", "expert"), 0, 0, tiled=True)
    grad_gate, grad_up, grad_down, grad_value = pl.pallas_call(
        lambda *refs: last_kernel(side_x, side_y, *refs),
        out_shape=(
            sds((own_rows, ff), F32),
            sds((own_rows, ff), F32),
            sds((own_rows, ff), F32),
            sds(shares.shape[1:], F32),
        ),
        compiler_params=params(),
        cost_estimate=cost(0, 24 * own_rows * ff),
        name="last",
    )(shares, firsts[0], *first_came, seconds[0], *second_came)
    return (grad_hidden, grad_route, grad_gate[None], grad_up[None], grad_down.T[None], grad_value)


def solution(mesh):
    pair = 2
    plane = mesh.shape["dp"] // pair
    side = math.isqrt(plane)
    grid = Mesh(mesh.devices.reshape(plane // side, side, pair, mesh.shape["expert"]), ALL)
    rows = P(ALL, None)
    dp = ("y", "x", "core")
    in_specs = (
        rows,
        rows,
        rows,
        rows,
        P(ALL),
        P(),
        P("expert", None, None),
        P("expert", None, None),
        P("expert", None, None),
        P(),
    )
    out_specs = (
        rows,
        rows,
        P("expert", dp, None),
        P("expert", dp, None),
        P("expert", None, dp),
        rows,
    )
    return jax.shard_map(
        per_device, mesh=grid, in_specs=in_specs, out_specs=out_specs, check_vma=False
    )
```

```python
import math

import jax
import jax.numpy as jnp
from jax import lax
from jax.experimental import pallas as pl
from jax.experimental.pallas import tpu as pltpu
from jax.sharding import Mesh, PartitionSpec as P

support_edge = 4.0
smoothing = 0.75
ALL = ("y", "x", "core", "expert")
BF16 = jnp.bfloat16
F32 = jnp.float32
STAT_ROWS = 16
MIB = 1024 * 1024
VMEM_BYTES = 62 * MIB


def dot(left, right, left_dim=1, right_dim=0):
    return lax.dot_general(
        left, right, (((left_dim,), (right_dim,)), ((), ())), preferred_element_type=F32
    )


def params():
    return pltpu.CompilerParams(vmem_limit_bytes=VMEM_BYTES)


def cost(flops, bytes_accessed):
    return pl.CostEstimate(flops=flops, bytes_accessed=bytes_accessed, transcendentals=0)


def whole(shape):
    return pl.BlockSpec(shape, lambda *_: (0,) * len(shape))


def pick(array, index, axis):
    return lax.dynamic_index_in_dim(array, index, axis, keepdims=False)


def swap_cores(array):
    return lax.ppermute(array, "core", [(0, 1), (1, 0)])


def send(arrays, axis_name):
    size = lax.axis_size(axis_name)
    came = {
        shift: lax.ppermute(
            arrays[shift], axis_name, [(k, (k + shift) % size) for k in range(size)]
        )
        for shift in sorted(range(1, size), key=lambda shift: -min(shift, size - shift))
    }
    return [came[shift] for shift in range(1, size)]


def summed(refs):
    total = refs[0][...].astype(F32)
    for ref in refs[1:]:
        total = total + ref[...].astype(F32)
    return total


def slots_kernel(groups, cap, ids_ref, hidden_ref, out_ref, slot_ref, any_ref):
    routes, tok_rows = ids_ref.shape
    ids = ids_ref[...]
    expert = lax.broadcasted_iota(jnp.int32, (8 * pl.cdiv(groups, 8), tok_rows), 0)
    named = [ids[k : k + 1, :] == expert for k in range(routes)]
    counts = sum(jnp.where(n, 1.0, 0.0) for n in named).astype(BF16)
    row = lax.broadcasted_iota(jnp.int32, (tok_rows, tok_rows), 0)
    col = lax.broadcasted_iota(jnp.int32, (tok_rows, tok_rows), 1)
    before = dot(counts, jnp.where(row < col, 1.0, 0.0).astype(BF16))
    slot_ids = lax.broadcasted_iota(jnp.int32, (groups * cap, tok_rows), 0)
    placed = jnp.zeros((groups * cap, tok_rows), F32)
    for k in range(routes):
        position = jnp.sum(jnp.where(named[k], before, 0.0), axis=0, keepdims=True)
        slot = ids[k : k + 1, :] * cap + position.astype(jnp.int32)
        placed = placed + jnp.where(slot_ids == slot, 1.0, 0.0)
        slot_ref[k : k + 1, :] = slot
    placed = placed.astype(BF16)
    any_ref[...] = placed
    width = hidden_ref.shape[1]
    step = min(512, width)
    for at in range(0, width, step):
        out_ref[:, at : at + step] = dot(placed, hidden_ref[:, at : at + step]).astype(BF16)


def front_kernel(
    cap, x_ref, gate_ref, up_ref, mix_ref, stat_ref, *refs
):
    act_ref, one_ref, two_ref, z_ref, acc = refs[-5:]
    step = pl.program_id(0)
    x = x_ref[...]
    gate = dot(x, gate_ref[...])
    up = dot(x, up_ref[...])
    sig = jax.nn.sigmoid(gate)
    act = (gate * sig * up).astype(BF16)
    act_ref[...] = act
    one_ref[...] = (up * sig * (1.0 + gate * (1.0 - sig))).astype(BF16)
    two_ref[...] = (gate * sig).astype(BF16)
    part = dot(act, mix_ref[...])

    @pl.when(step == 0)
    def _():
        acc[...] = part

    @pl.when(step > 0)
    def _():
        acc[...] += part

    @pl.when(step == pl.num_programs(0) - 1)
    def _():
        total = acc[...].astype(BF16)
        shape = (STAT_ROWS, z_ref.shape[2])
        lane = lax.broadcasted_iota(jnp.int32, shape, 1)
        stat = jnp.where(lane < shape[1] // 2, stat_ref[0], stat_ref[1])
        high = stat.astype(BF16).astype(F32)
        middle = (stat - high).astype(BF16).astype(F32)
        low = stat - high - middle
        row = lax.broadcasted_iota(jnp.int32, stat.shape, 0)
        rows = jnp.where(
            row == 0, high, jnp.where(row == 1, middle, jnp.where(row == 2, low, 0.0))
        ).astype(BF16)
        for group in range(z_ref.shape[0]):
            z_ref[group, :cap, :] = total[group * cap : (group + 1) * cap]
            z_ref[group, cap:, :] = rows


def head_kernel(
    cap, token_count, moments_ref, back_ref, slot_ref, weight_ref, resid_ref, returns_ref, *refs
):
    out_ref, grad_ref, route_ref = refs[-3:]
    groups, _, bins = back_ref.shape
    routes, tok_rows = slot_ref.shape
    stat = jnp.sum(jnp.sum(back_ref[:, cap:, :].astype(F32), axis=0), axis=0, keepdims=True)
    half = bins // 2
    batch_mean = stat[:, 0:1] / token_count
    batch_var = stat[:, half : half + 1] / token_count - batch_mean * batch_mean
    run_mean, run_var = moments_ref[0], moments_ref[1]
    mean_value = 0.5 * (run_mean + batch_mean)
    var_value = 0.5 * (run_var + batch_var) + 0.25 * (batch_mean - run_mean) ** 2
    scaled = jnp.clip(
        (returns_ref[...] - mean_value) / jnp.sqrt(var_value + 1e-06), -support_edge, support_edge
    )
    width = 2.0 * support_edge / bins
    scale = math.sqrt(2.0) * smoothing * width
    edge = lax.broadcasted_iota(jnp.int32, (tok_rows, bins), 1).astype(F32) * width - support_edge
    lower = lax.erf((edge - scaled) / scale)
    upper = lax.erf((edge + width - scaled) / scale)
    targets = (upper - lower) / (upper[:, bins - 1 :] - lower[:, :1])

    back = jnp.concatenate([back_ref[group, :cap, :] for group in range(groups)], axis=0)
    slot_ids = lax.broadcasted_iota(jnp.int32, (groups * cap, tok_rows), 0)
    placed, token_logits = [], []
    logits = resid_ref[...]
    for k in range(routes):
        placed.append(jnp.where(slot_ids == slot_ref[k : k + 1, :], 1.0, 0.0).astype(BF16))
        token_logits.append(dot(placed[k], back, 0, 0))
        logits = logits + weight_ref[:, k : k + 1] * token_logits[k]
    power = jnp.exp(logits - jnp.max(logits, axis=1, keepdims=True))
    probs = power / jnp.sum(power, axis=1, keepdims=True)
    grad = (probs - targets).astype(BF16)
    grad_ref[...] = grad
    grad_f = grad.astype(F32)
    total = jnp.zeros((groups * cap, bins), F32)
    which = lax.broadcasted_iota(jnp.int32, (tok_rows, routes), 1)
    route = jnp.zeros((tok_rows, routes), F32)
    for k in range(routes):
        weighted = (weight_ref[:, k : k + 1] * grad_f).astype(BF16)
        total = total + dot(placed[k], weighted)
        sums = jnp.sum(token_logits[k] * grad_f, axis=1, keepdims=True)
        route = jnp.where(which == k, sums, route)
    out_ref[...] = total.astype(BF16)
    route_ref[...] = route


def back_kernel(grad_ref, mix_ref, one_ref, two_ref, gate_ref, up_ref, *refs):
    input_ref, pair_ref = refs[-2:]
    ff = one_ref.shape[1]

    @pl.when(pl.program_id(0) == 0)
    def _():
        act_grad = dot(grad_ref[...], mix_ref[...], 1, 1)
        pair_ref[:, :ff] = (act_grad * one_ref[...].astype(F32)).astype(BF16)
        pair_ref[:, ff:] = (act_grad * two_ref[...].astype(F32)).astype(BF16)

    input_ref[...] = (
        dot(pair_ref[:, :ff], gate_ref[...], 1, 1) + dot(pair_ref[:, ff:], up_ref[...], 1, 1)
    ).astype(BF16)


def far_kernel(
    coord_ref, rows_x, rows_x2, resid_x, resid_x2, down_x, value_x, rows_y, rows_y2, value_y, pair_ref,
    grad_ref, grad2_ref, row_grad, row_grad2, mix_ref, one2_ref, two2_ref, act_ref, act2_ref,
    first_ref, second_ref, pair2_ref, inner_ref,
):
    ff = act_ref.shape[1]
    act_grad = dot(row_grad2[...], mix_ref[...], 1, 1)
    pair2_ref[:, :ff] = (act_grad * one2_ref[...].astype(F32)).astype(BF16)
    pair2_ref[:, ff:] = (act_grad * two2_ref[...].astype(F32)).astype(BF16)
    inner_ref[...] = (
        dot(act_ref[...], row_grad[...], 0, 0) + dot(act2_ref[...], row_grad2[...], 0, 0)
    ).astype(BF16)
    gates, ups = slice(None, ff), slice(ff, None)
    x_kernel(
        1, coord_ref, rows_x, rows_x2, resid_x, resid_x2, down_x, value_x, pair_ref.at[:, gates],
        pair2_ref.at[:, gates], inner_ref, grad_ref, grad2_ref, first_ref,
    )
    y_kernel(
        1, coord_ref, rows_y, rows_y2, value_y, pair_ref.at[:, ups], pair2_ref.at[:, ups],
        inner_ref, second_ref,
    )


def own_kernel(
    coord_ref, rows_x, rows_x2, resid_x, resid_x2, down_x, value_x, rows_y, rows_y2, value_y, pair_ref,
    pair2_ref, inner_ref, grad_ref, grad2_ref, *refs,
):
    first_ref, second_ref = refs[-2:]
    ff = inner_ref.shape[0]
    gates, ups = slice(None, ff), slice(ff, None)
    x_kernel(
        1, coord_ref, rows_x, rows_x2, resid_x, resid_x2, down_x, value_x, pair_ref.at[:, gates],
        pair2_ref.at[:, gates], inner_ref, grad_ref, grad2_ref, first_ref,
    )
    y_kernel(
        1, coord_ref, rows_y, rows_y2, value_y, pair_ref.at[:, ups], pair2_ref.at[:, ups],
        inner_ref, second_ref,
    )


def flat(ref):
    return ref[...].reshape(ref.shape[0] * ref.shape[1] * ref.shape[2], ref.shape[3])


def write(outs, at, value):
    for number, out in enumerate(outs):

        def put():
            shape = out.shape[:2] + (value.shape[1],)
            out[:, :, at : at + value.shape[1]] = value.reshape(shape).astype(out.dtype)

        if len(outs) == 1:
            put()
        else:
            pl.when(pl.program_id(0) == number)(put)


def x_kernel(
    count, coord_ref, rows_x, rows_x2, resid_x, resid_x2, down_x, value_x, pair_ref, pair2_ref,
    inner_ref, grad_ref, grad2_ref, *outs,
):
    del coord_ref
    outs = outs[-count:]
    write(outs, 0, dot(flat(rows_x), pair_ref[...]) + dot(flat(rows_x2), pair2_ref[...]))
    ff = inner_ref.shape[0]
    cut = ff // 6
    write(outs, ff, dot(flat(value_x), inner_ref[:cut, :], 1, 1))
    write(
        outs,
        ff + cut,
        dot(flat(resid_x), grad_ref[...])
        + dot(flat(resid_x2), grad2_ref[...])
        + dot(flat(down_x), inner_ref[...]),
    )


def y_kernel(
    count, coord_ref, rows_y, rows_y2, value_y, pair_ref, pair2_ref, inner_ref, *outs
):
    del coord_ref
    outs = outs[-count:]
    write(outs, 0, dot(flat(rows_y), pair_ref[...]) + dot(flat(rows_y2), pair2_ref[...]))
    ff = inner_ref.shape[0]
    write(outs, ff, dot(flat(value_y), inner_ref[ff // 6 :, :], 1, 1))


def pass_kernel(head_ref, token, out_ref):
    del token
    out_ref[...] = head_ref[...]


def summed_at(refs, index, columns):
    total = refs[0][index, :, columns].astype(F32)
    for ref in refs[1:]:
        total = total + ref[index, :, columns].astype(F32)
    return total


def first_kernel(coord_ref, *refs):
    parts, (head_ref, *outs) = refs[:4], refs[-5:]
    side, columns = len(outs), outs[0].shape[1]
    for y in range(side):
        head_ref[y] = summed_at(parts, y, slice(columns, None))
    for shift, out in enumerate(outs):
        y = lax.rem(coord_ref[1] + shift, side)
        out[...] = summed_at(parts, y, slice(None, columns)).astype(out.dtype)


def second_kernel(coord_ref, *refs):
    parts, outs = refs[:4], refs[-4:]
    for shift, out in enumerate(outs):
        x = lax.rem(coord_ref[0] + shift, len(outs))
        out[...] = summed_at(parts, x, slice(None)).astype(out.dtype)


def last_kernel(side_x, side_y, head_ref, *refs):
    firsts, seconds = refs[:side_y], refs[side_y : side_y + side_x]
    gate_ref, up_ref, down_ref, value_ref = refs[side_y + side_x :]
    ff = gate_ref.shape[1]
    first, second = summed(firsts), summed(seconds)
    cut = first.shape[1] - ff
    gate_ref[...] = first[:, :ff]
    up_ref[...] = second[:, :ff]
    down_ref[:, :cut] = first[:, ff:]
    down_ref[:, cut:] = second[:, ff:]
    value_ref[...] = jnp.sum(head_ref[...], axis=0)


def turn_kernel(core_ref, rows_ref, token, mine_ref, other_ref):
    del token
    own = mine_ref.shape[1]
    for at in range(mine_ref.shape[0]):
        turned = rows_ref[:, 2 * own * at : 2 * own * (at + 1)].T
        low, high = turned[:own], turned[own:]
        mine_ref[at] = jnp.where(core_ref[0] == 0, low, high)
        other_ref[at] = jnp.where(core_ref[0] == 0, high, low)


def per_shift(count, shape):
    return tuple(jax.ShapeDtypeStruct(shape, BF16 if shift else F32) for shift in range(count))


def per_device(
    hidden_in,
    resid_in,
    route_ids,
    route_weight,
    returns,
    run_moments,
    gate_w,
    up_w,
    down_w,
    value_w,
):
    groups = lax.axis_size("expert")
    side_y, side_x = lax.axis_size("y"), lax.axis_size("x")
    core = lax.axis_index("core")
    tok_rows, width = hidden_in.shape
    routes = route_ids.shape[1]
    cap = 3 * tok_rows * routes // (2 * groups)
    slot_total = groups * cap
    bins = value_w.shape[1]
    gate_w, up_w, down_w = gate_w[0], up_w[0], down_w[0]
    ff = gate_w.shape[1]
    own_rows = width // (side_y * side_x * 2)
    token_count = float(tok_rows * groups * side_y * side_x * 2)
    sds = jax.ShapeDtypeStruct
    anywhere = pl.BlockSpec(memory_space=pl.ANY)
    smem = pl.BlockSpec(memory_space=pltpu.SMEM)
    vmem = pl.BlockSpec(memory_space=pltpu.VMEM)

    coords = jnp.stack([lax.axis_index("x"), lax.axis_index("y")]).astype(jnp.int32)

    def core_half(array):
        blocks = array.reshape(side_y * side_x, 2, own_rows, array.shape[1])
        mine = pick(blocks, core, 1).reshape(width // 2, array.shape[1])
        other = pick(blocks, 1 - core, 1).reshape(width // 2, array.shape[1])
        return mine, other

    def exchange(blocks):
        return lax.all_to_all(blocks, "expert", 0, 0, tiled=True)

    def exchange_rows(rows):
        return exchange(rows.reshape(groups, cap, rows.shape[1])).reshape(rows.shape)

    outgoing, slots, placed_any = pl.pallas_call(
        lambda *refs: slots_kernel(groups, cap, *refs),
        out_shape=(
            sds((slot_total, width), BF16),
            sds((routes, tok_rows), jnp.int32),
            sds((slot_total, tok_rows), BF16),
        ),
        compiler_params=params(),
        cost_estimate=cost(2 * tok_rows * slot_total * width, 2 * width * (slot_total + tok_rows)),
        name="slots",
    )(route_ids.T, hidden_in)
    in_rows = exchange_rows(outgoing)

    with jax.named_scope("moments"):
        sums = jnp.stack([jnp.sum(returns), jnp.sum(returns * returns)])
        for axis_name in ("x", "y", "core"):
            sums = lax.psum(sums, axis_name)

    with jax.named_scope("weights_only"):
        mix = dot(down_w, value_w).astype(BF16)
        resid_logits = dot(resid_in, value_w)
        value_mine, _ = core_half(value_w)
        down_mine, _ = core_half(down_w.T)
        resid_mine, resid_other = core_half(resid_in.T)
        resid_peer = swap_cores(resid_other)

    steps = 1
    part = ff // steps
    act, one, two, route_logits = pl.pallas_call(
        lambda *refs: front_kernel(cap, *refs),
        grid=(steps,),
        in_specs=[
            whole((slot_total, width)),
            pl.BlockSpec((width, part), lambda j: (0, j)),
            pl.BlockSpec((width, part), lambda j: (0, j)),
            pl.BlockSpec((part, bins), lambda j: (j, 0)),
            smem,
        ]
        + [anywhere] * 4,
        out_specs=[
            pl.BlockSpec((slot_total, part), lambda j: (0, j)),
            pl.BlockSpec((slot_total, part), lambda j: (0, j)),
            pl.BlockSpec((slot_total, part), lambda j: (0, j)),
            whole((groups, cap + STAT_ROWS, bins)),
        ],
        out_shape=(
            sds((slot_total, ff), BF16),
            sds((slot_total, ff), BF16),
            sds((slot_total, ff), BF16),
            sds((groups, cap + STAT_ROWS, bins), BF16),
        ),
        scratch_shapes=[pltpu.VMEM((slot_total, bins), F32)],
        compiler_params=params(),
        cost_estimate=cost(4 * slot_total * width * ff, 4 * width * ff),
        name="front",
    )(in_rows, gate_w, up_w, mix, sums, value_mine, down_mine, resid_mine, resid_peer)
    back_logits = exchange(route_logits)
    with jax.named_scope("turned"):
        chips = side_y * side_x
        rows_mine, rows_other = pl.pallas_call(
            turn_kernel,
            grid=(4,),
            in_specs=[
                smem,
                pl.BlockSpec((slot_total, width // 4), lambda i: (0, i)),
                anywhere,
            ],
            out_specs=[pl.BlockSpec((chips // 4, own_rows, slot_total), lambda i: (i, 0, 0))] * 2,
            out_shape=(sds((chips, own_rows, slot_total), BF16),) * 2,
            compiler_params=params(),
            cost_estimate=cost(0, 4 * slot_total * width),
            name="turn",
        )(core.astype(jnp.int32)[None], in_rows, act)
        rows_mine = rows_mine.reshape(width // 2, slot_total)
        rows_peer = swap_cores(rows_other).reshape(width // 2, slot_total)
        act_peer, one_peer, two_peer = swap_cores(act), swap_cores(one), swap_cores(two)

    out_grad, logit_grad, grad_route = pl.pallas_call(
        lambda *refs: head_kernel(cap, token_count, *refs),
        in_specs=[smem]
        + [vmem] * 5
        + [anywhere] * 2
        + [smem],
        out_shape=(
            sds((slot_total, bins), BF16),
            sds((tok_rows, bins), BF16),
            sds((tok_rows, routes), F32),
        ),
        compiler_params=params(),
        cost_estimate=cost(8 * tok_rows * slot_total * bins, 4 * slot_total * bins),
        name="head",
    )(
        run_moments, back_logits, slots, route_weight, resid_logits, returns.reshape(tok_rows, 1),
        rows_mine, rows_other, coords,
    )
    row_grad = exchange_rows(out_grad)
    grad_peer = swap_cores(logit_grad)

    row_grad_peer = swap_cores(row_grad)

    strip = min(1024, width)
    input_grad, pair = pl.pallas_call(
        back_kernel,
        grid=(width // strip,),
        in_specs=[
            whole((slot_total, bins)),
            whole((ff, bins)),
            whole((slot_total, ff)),
            whole((slot_total, ff)),
            pl.BlockSpec((strip, ff), lambda i: (i, 0)),
            pl.BlockSpec((strip, ff), lambda i: (i, 0)),
        ]
        + [anywhere] * 5,
        out_specs=[
            pl.BlockSpec((slot_total, strip), lambda i: (0, i)),
            whole((slot_total, 2 * ff)),
        ],
        out_shape=(
            sds((slot_total, width), BF16),
            sds((slot_total, 2 * ff), BF16),
        ),
        compiler_params=params(),
        cost_estimate=cost(4 * slot_total * width * ff, 4 * width * ff),
        name="back",
    )(
        row_grad, mix, one, two, gate_w, up_w, rows_peer, grad_peer, act_peer, one_peer, two_peer
    )
    back_grad = exchange_rows(input_grad)

    half = width // 2
    cut = ff // 6
    first_columns, second_columns = ff + cut + bins, 2 * ff - cut
    first_block, second_block = (side_y, own_rows, first_columns), (side_x, own_rows, second_columns)

    def parts(kernel, shifts, blocked, shared, outs, name):
        def shift_of(step):
            return shifts[0] if len(shifts) == 1 else shifts[0] + step * (shifts[1] - shifts[0])

        def tall(depth):
            return pl.BlockSpec(
                (side_y, 1, own_rows, depth),
                lambda step, at: (0, lax.rem(at[0] + shift_of(step), side_x), 0, 0),
            )

        def wide(depth):
            return pl.BlockSpec(
                (1, side_x, own_rows, depth),
                lambda step, at: (lax.rem(at[1] + shift_of(step), side_y), 0, 0, 0),
            )

        makes = {"x": tall, "y": wide}
        return pl.pallas_call(
            kernel,
            grid_spec=pltpu.PrefetchScalarGridSpec(
                num_scalar_prefetch=1,
                grid=(len(shifts),),
                in_specs=[makes[along](rows.shape[1]) for along, rows in blocked]
                + [whole(item.shape) if spec is None else spec for spec, item in shared],
                out_specs=[whole(out.shape) for out in outs],
            ),
            out_shape=outs,
            compiler_params=params(),
            cost_estimate=cost(len(shifts) * half * slot_total * ff, len(shifts) * 3 * MIB),
            name=name,
        )(
            coords,
            *[rows.reshape(side_y, side_x, own_rows, rows.shape[1]) for _, rows in blocked],
            *[item for _, item in shared],
        )

    def step_on(array, axis_name, shift):
        size = lax.axis_size(axis_name)
        return lax.ppermute(array, axis_name, [(k, (k + shift) % size) for k in range(size)])

    x_rows = [
        ("x", r) for r in (rows_mine, rows_peer, resid_mine, resid_peer, down_mine, value_mine)
    ]
    y_rows = [("y", r) for r in (rows_mine, rows_peer, value_mine)]
    first_out, second_out = sds(first_block, BF16), sds(second_block, BF16)
    first_far, second_far, pair_peer, inner = parts(
        far_kernel,
        (2,),
        x_rows + y_rows,
        [
            (None, item)
            for item in (
                pair, logit_grad, grad_peer, row_grad, row_grad_peer, mix, one_peer, two_peer,
                act, act_peer,
            )
        ],
        [first_out, second_out, sds(pair.shape, BF16), sds((ff, bins), BF16)],
        "far",
    )
    gate_spec = pl.BlockSpec((slot_total, ff), lambda *_: (0, 0))
    up_spec = pl.BlockSpec((slot_total, ff), lambda *_: (0, 1))

    firsts = [step_on(first_far, "x", 2)]
    seconds = [step_on(second_far, "y", 2)]
    first_up, first_down = parts(
        lambda *refs: x_kernel(2, *refs),
        (1, 3),
        x_rows,
        [
            (gate_spec, pair), (gate_spec, pair_peer), (None, inner), (None, logit_grad),
            (None, grad_peer),
        ],
        [first_out] * 2,
        "x_near",
    )
    firsts += [step_on(first_up, "x", 1), step_on(first_down, "x", 3)]
    second_up, second_down = parts(
        lambda *refs: y_kernel(2, *refs),
        (1, 3),
        y_rows,
        [
            (up_spec, pair), (up_spec, pair_peer), (None, inner), (anywhere, first_up),
        ],
        [second_out] * 2,
        "y_near",
    )
    first_own, second_own = parts(
        own_kernel,
        (0,),
        x_rows + y_rows,
        [
            (None, pair), (None, pair_peer), (None, inner), (None, logit_grad), (None, grad_peer),
            (anywhere, second_up), (anywhere, seconds[0]), (anywhere, firsts[0]),
        ],
        [first_out, second_out],
        "own",
    )
    seconds += [step_on(second_up, "y", 1), step_on(second_down, "y", 3)]

    head, *firsts = pl.pallas_call(
        first_kernel,
        in_specs=[smem] + [vmem] * 4,
        out_shape=(sds((side_y, own_rows, bins), F32),)
        + per_shift(side_y, (own_rows, first_columns - bins)),
        compiler_params=params(),
        cost_estimate=cost(0, 12 * side_y * own_rows * ff),
        name="first",
    )(coords, first_own, *firsts)
    first_came = send(firsts, "y")
    seconds = pl.pallas_call(
        second_kernel,
        in_specs=[smem] + [vmem] * 4,
        out_shape=per_shift(side_x, (own_rows, second_columns)),
        compiler_params=params(),
        cost_estimate=cost(0, 24 * side_y * own_rows * ff),
        name="second",
    )(coords, second_own, *seconds)
    second_came = send(seconds, "x")
    with jax.named_scope("hidden"):
        grad_hidden = dot(placed_any, back_grad, 0, 0).astype(BF16)
    head = pl.pallas_call(
        pass_kernel,
        in_specs=[vmem, anywhere],
        out_shape=sds(head.shape, F32),
        compiler_params=params(),
        cost_estimate=cost(0, 8 * side_y * own_rows * bins),
        name="pass",
    )(head, back_grad)
    shares = head.reshape(side_y * groups, own_rows // groups, bins)
    shares = lax.all_to_all(shares, ("y", "expert"), 0, 0, tiled=True)
    grad_gate, grad_up, grad_down, grad_value = pl.pallas_call(
        lambda *refs: last_kernel(side_x, side_y, *refs),
        out_shape=(
            sds((own_rows, ff), F32),
            sds((own_rows, ff), F32),
            sds((own_rows, ff), F32),
            sds(shares.shape[1:], F32),
        ),
        compiler_params=params(),
        cost_estimate=cost(0, 24 * own_rows * ff),
        name="last",
    )(shares, firsts[0], *first_came, seconds[0], *second_came)
    return (grad_hidden, grad_route, grad_gate[None], grad_up[None], grad_down.T[None], grad_value)


def solution(mesh):
    pair = 2
    plane = mesh.shape["dp"] // pair
    side = math.isqrt(plane)
    grid = Mesh(mesh.devices.reshape(plane // side, side, pair, mesh.shape["expert"]), ALL)
    rows = P(ALL, None)
    dp = ("y", "x", "core")
    in_specs = (
        rows,
        rows,
        rows,
        rows,
        P(ALL),
        P(),
        P("expert", None, None),
        P("expert", None, None),
        P("expert", None, None),
        P(),
    )
    out_specs = (
        rows,
        rows,
        P("expert", dp, None),
        P("expert", dp, None),
        P("expert", None, dp),
        rows,
    )
    return jax.shard_map(
        per_device, mesh=grid, in_specs=in_specs, out_specs=out_specs, check_vma=False
    )
```

```python
import math

import jax
import jax.numpy as jnp
from jax import lax
from jax.experimental import pallas as pl
from jax.experimental.pallas import tpu as pltpu
from jax.sharding import Mesh, PartitionSpec as P

support_edge = 4.0
smoothing = 0.75
ALL = ("y", "x", "core", "expert")
BF16 = jnp.bfloat16
F32 = jnp.float32
STAT_ROWS = 16
MIB = 1024 * 1024
VMEM_BYTES = 62 * MIB


def dot(left, right, left_dim=1, right_dim=0):
    return lax.dot_general(
        left, right, (((left_dim,), (right_dim,)), ((), ())), preferred_element_type=F32
    )


def params():
    return pltpu.CompilerParams(vmem_limit_bytes=VMEM_BYTES)


def cost(flops, bytes_accessed):
    return pl.CostEstimate(flops=flops, bytes_accessed=bytes_accessed, transcendentals=0)


def whole(shape):
    return pl.BlockSpec(shape, lambda *_: (0,) * len(shape))


def pick(array, index, axis):
    return lax.dynamic_index_in_dim(array, index, axis, keepdims=False)


def swap_cores(array):
    return lax.ppermute(array, "core", [(0, 1), (1, 0)])


def send(arrays, axis_name):
    size = lax.axis_size(axis_name)
    came = {
        shift: lax.ppermute(
            arrays[shift], axis_name, [(k, (k + shift) % size) for k in range(size)]
        )
        for shift in sorted(range(1, size), key=lambda shift: -min(shift, size - shift))
    }
    return [came[shift] for shift in range(1, size)]


def summed(refs):
    total = refs[0][...].astype(F32)
    for ref in refs[1:]:
        total = total + ref[...].astype(F32)
    return total


def slots_kernel(groups, cap, ids_ref, hidden_ref, out_ref, slot_ref, any_ref):
    routes, tok_rows = ids_ref.shape
    ids = ids_ref[...]
    expert = lax.broadcasted_iota(jnp.int32, (8 * pl.cdiv(groups, 8), tok_rows), 0)
    named = [ids[k : k + 1, :] == expert for k in range(routes)]
    counts = sum(jnp.where(n, 1.0, 0.0) for n in named).astype(BF16)
    row = lax.broadcasted_iota(jnp.int32, (tok_rows, tok_rows), 0)
    col = lax.broadcasted_iota(jnp.int32, (tok_rows, tok_rows), 1)
    before = dot(counts, jnp.where(row < col, 1.0, 0.0).astype(BF16))
    slot_ids = lax.broadcasted_iota(jnp.int32, (groups * cap, tok_rows), 0)
    placed = jnp.zeros((groups * cap, tok_rows), F32)
    for k in range(routes):
        position = jnp.sum(jnp.where(named[k], before, 0.0), axis=0, keepdims=True)
        slot = ids[k : k + 1, :] * cap + position.astype(jnp.int32)
        placed = placed + jnp.where(slot_ids == slot, 1.0, 0.0)
        slot_ref[k : k + 1, :] = slot
    placed = placed.astype(BF16)
    any_ref[...] = placed
    width = hidden_ref.shape[1]
    step = min(512, width)
    for at in range(0, width, step):
        out_ref[:, at : at + step] = dot(placed, hidden_ref[:, at : at + step]).astype(BF16)


def front_kernel(
    cap, x_ref, gate_ref, up_ref, mix_ref, stat_ref, *refs
):
    act_ref, one_ref, two_ref, z_ref, acc = refs[-5:]
    step = pl.program_id(0)
    x = x_ref[...]
    gate = dot(x, gate_ref[...])
    up = dot(x, up_ref[...])
    sig = jax.nn.sigmoid(gate)
    act = (gate * sig * up).astype(BF16)
    act_ref[...] = act
    one_ref[...] = (up * sig * (1.0 + gate * (1.0 - sig))).astype(BF16)
    two_ref[...] = (gate * sig).astype(BF16)
    part = dot(act, mix_ref[...])

    @pl.when(step == 0)
    def _():
        acc[...] = part

    @pl.when(step > 0)
    def _():
        acc[...] += part

    @pl.when(step == pl.num_programs(0) - 1)
    def _():
        total = acc[...].astype(BF16)
        shape = (STAT_ROWS, z_ref.shape[2])
        lane = lax.broadcasted_iota(jnp.int32, shape, 1)
        stat = jnp.where(lane < shape[1] // 2, stat_ref[0], stat_ref[1])
        high = stat.astype(BF16).astype(F32)
        middle = (stat - high).astype(BF16).astype(F32)
        low = stat - high - middle
        row = lax.broadcasted_iota(jnp.int32, stat.shape, 0)
        rows = jnp.where(
            row == 0, high, jnp.where(row == 1, middle, jnp.where(row == 2, low, 0.0))
        ).astype(BF16)
        for group in range(z_ref.shape[0]):
            z_ref[group, :cap, :] = total[group * cap : (group + 1) * cap]
            z_ref[group, cap:, :] = rows


def head_kernel(
    cap, token_count, moments_ref, back_ref, slot_ref, weight_ref, resid_ref, returns_ref, *refs
):
    out_ref, grad_ref, route_ref = refs[-3:]
    groups, _, bins = back_ref.shape
    routes, tok_rows = slot_ref.shape
    stat = jnp.sum(jnp.sum(back_ref[:, cap:, :].astype(F32), axis=0), axis=0, keepdims=True)
    half = bins // 2
    batch_mean = stat[:, 0:1] / token_count
    batch_var = stat[:, half : half + 1] / token_count - batch_mean * batch_mean
    run_mean, run_var = moments_ref[0], moments_ref[1]
    mean_value = 0.5 * (run_mean + batch_mean)
    var_value = 0.5 * (run_var + batch_var) + 0.25 * (batch_mean - run_mean) ** 2
    scaled = jnp.clip(
        (returns_ref[...] - mean_value) / jnp.sqrt(var_value + 1e-06), -support_edge, support_edge
    )
    width = 2.0 * support_edge / bins
    scale = math.sqrt(2.0) * smoothing * width
    edge = lax.broadcasted_iota(jnp.int32, (tok_rows, bins), 1).astype(F32) * width - support_edge
    lower = lax.erf((edge - scaled) / scale)
    upper = lax.erf((edge + width - scaled) / scale)
    targets = (upper - lower) / (upper[:, bins - 1 :] - lower[:, :1])

    back = jnp.concatenate([back_ref[group, :cap, :] for group in range(groups)], axis=0)
    slot_ids = lax.broadcasted_iota(jnp.int32, (groups * cap, tok_rows), 0)
    placed, token_logits = [], []
    logits = resid_ref[...]
    for k in range(routes):
        placed.append(jnp.where(slot_ids == slot_ref[k : k + 1, :], 1.0, 0.0).astype(BF16))
        token_logits.append(dot(placed[k], back, 0, 0))
        logits = logits + weight_ref[:, k : k + 1] * token_logits[k]
    power = jnp.exp(logits - jnp.max(logits, axis=1, keepdims=True))
    probs = power / jnp.sum(power, axis=1, keepdims=True)
    grad = (probs - targets).astype(BF16)
    grad_ref[...] = grad
    grad_f = grad.astype(F32)
    total = jnp.zeros((groups * cap, bins), F32)
    which = lax.broadcasted_iota(jnp.int32, (tok_rows, routes), 1)
    route = jnp.zeros((tok_rows, routes), F32)
    for k in range(routes):
        weighted = (weight_ref[:, k : k + 1] * grad_f).astype(BF16)
        total = total + dot(placed[k], weighted)
        sums = jnp.sum(token_logits[k] * grad_f, axis=1, keepdims=True)
        route = jnp.where(which == k, sums, route)
    out_ref[...] = total.astype(BF16)
    route_ref[...] = route


def back_kernel(grad_ref, mix_ref, one_ref, two_ref, gate_ref, up_ref, *refs):
    input_ref, pair_ref = refs[-2:]
    ff = one_ref.shape[1]

    @pl.when(pl.program_id(0) == 0)
    def _():
        act_grad = dot(grad_ref[...], mix_ref[...], 1, 1)
        pair_ref[:, :ff] = (act_grad * one_ref[...].astype(F32)).astype(BF16)
        pair_ref[:, ff:] = (act_grad * two_ref[...].astype(F32)).astype(BF16)

    input_ref[...] = (
        dot(pair_ref[:, :ff], gate_ref[...], 1, 1) + dot(pair_ref[:, ff:], up_ref[...], 1, 1)
    ).astype(BF16)


def far_kernel(
    coord_ref, rows_x, rows_x2, resid_x, resid_x2, down_x, value_x, rows_y, rows_y2, value_y, pair_ref,
    grad_ref, grad2_ref, row_grad, row_grad2, mix_ref, one2_ref, two2_ref, act_ref, act2_ref,
    first_ref, second_ref, pair2_ref, inner_ref,
):
    ff = act_ref.shape[1]
    act_grad = dot(row_grad2[...], mix_ref[...], 1, 1)
    pair2_ref[:, :ff] = (act_grad * one2_ref[...].astype(F32)).astype(BF16)
    pair2_ref[:, ff:] = (act_grad * two2_ref[...].astype(F32)).astype(BF16)
    inner_ref[...] = (
        dot(act_ref[...], row_grad[...], 0, 0) + dot(act2_ref[...], row_grad2[...], 0, 0)
    ).astype(BF16)
    gates, ups = slice(None, ff), slice(ff, None)
    x_kernel(
        1, coord_ref, rows_x, rows_x2, resid_x, resid_x2, down_x, value_x, pair_ref.at[:, gates],
        pair2_ref.at[:, gates], inner_ref, grad_ref, grad2_ref, first_ref,
    )
    y_kernel(
        1, coord_ref, rows_y, rows_y2, value_y, pair_ref.at[:, ups], pair2_ref.at[:, ups],
        inner_ref, second_ref,
    )


def own_kernel(
    coord_ref, rows_x, rows_x2, resid_x, resid_x2, down_x, value_x, rows_y, rows_y2, value_y, pair_ref,
    pair2_ref, inner_ref, grad_ref, grad2_ref, *refs,
):
    first_ref, second_ref = refs[-2:]
    ff = inner_ref.shape[0]
    gates, ups = slice(None, ff), slice(ff, None)
    x_kernel(
        1, coord_ref, rows_x, rows_x2, resid_x, resid_x2, down_x, value_x, pair_ref.at[:, gates],
        pair2_ref.at[:, gates], inner_ref, grad_ref, grad2_ref, first_ref,
    )
    y_kernel(
        1, coord_ref, rows_y, rows_y2, value_y, pair_ref.at[:, ups], pair2_ref.at[:, ups],
        inner_ref, second_ref,
    )


def flat(ref):
    return ref[...].reshape(ref.shape[0] * ref.shape[1] * ref.shape[2], ref.shape[3])


def write(outs, at, value):
    for number, out in enumerate(outs):

        def put():
            shape = out.shape[:2] + (value.shape[1],)
            out[:, :, at : at + value.shape[1]] = value.reshape(shape).astype(out.dtype)

        if len(outs) == 1:
            put()
        else:
            pl.when(pl.program_id(0) == number)(put)


def x_kernel(
    count, coord_ref, rows_x, rows_x2, resid_x, resid_x2, down_x, value_x, pair_ref, pair2_ref,
    inner_ref, grad_ref, grad2_ref, *outs,
):
    del coord_ref
    outs = outs[-count:]
    write(outs, 0, dot(flat(rows_x), pair_ref[...]) + dot(flat(rows_x2), pair2_ref[...]))
    ff = inner_ref.shape[0]
    cut = ff // 6
    write(outs, ff, dot(flat(value_x), inner_ref[:cut, :], 1, 1))
    write(
        outs,
        ff + cut,
        dot(flat(resid_x), grad_ref[...])
        + dot(flat(resid_x2), grad2_ref[...])
        + dot(flat(down_x), inner_ref[...]),
    )


def y_kernel(
    count, coord_ref, rows_y, rows_y2, value_y, pair_ref, pair2_ref, inner_ref, *outs
):
    del coord_ref
    outs = outs[-count:]
    write(outs, 0, dot(flat(rows_y), pair_ref[...]) + dot(flat(rows_y2), pair2_ref[...]))
    ff = inner_ref.shape[0]
    write(outs, ff, dot(flat(value_y), inner_ref[ff // 6 :, :], 1, 1))


def pass_kernel(head_ref, token, out_ref):
    del head_ref, token, out_ref


def summed_at(refs, index, columns):
    total = refs[0][index, :, columns].astype(F32)
    for ref in refs[1:]:
        total = total + ref[index, :, columns].astype(F32)
    return total


def first_kernel(coord_ref, *refs):
    parts, (head_ref, *outs) = refs[:4], refs[-5:]
    side, columns = len(outs), outs[0].shape[1]
    for y in range(side):
        head_ref[y] = summed_at(parts, y, slice(columns, None))
    for shift, out in enumerate(outs):
        y = lax.rem(coord_ref[1] + shift, side)
        out[...] = summed_at(parts, y, slice(None, columns)).astype(out.dtype)


def second_kernel(coord_ref, *refs):
    parts, outs = refs[:4], refs[-4:]
    for shift, out in enumerate(outs):
        x = lax.rem(coord_ref[0] + shift, len(outs))
        out[...] = summed_at(parts, x, slice(None)).astype(out.dtype)


def last_kernel(side_x, side_y, head_ref, *refs):
    firsts, seconds = refs[:side_y], refs[side_y : side_y + side_x]
    gate_ref, up_ref, down_ref, value_ref = refs[side_y + side_x :]
    ff = gate_ref.shape[1]
    first, second = summed(firsts), summed(seconds)
    cut = first.shape[1] - ff
    gate_ref[...] = first[:, :ff]
    up_ref[...] = second[:, :ff]
    down_ref[:, :cut] = first[:, ff:]
    down_ref[:, cut:] = second[:, ff:]
    value_ref[...] = jnp.sum(head_ref[...], axis=0)


def turn_kernel(core_ref, rows_ref, token, mine_ref, other_ref):
    del token
    own = mine_ref.shape[1]
    for at in range(mine_ref.shape[0]):
        turned = rows_ref[:, 2 * own * at : 2 * own * (at + 1)].T
        low, high = turned[:own], turned[own:]
        mine_ref[at] = jnp.where(core_ref[0] == 0, low, high)
        other_ref[at] = jnp.where(core_ref[0] == 0, high, low)


def per_shift(count, shape):
    return tuple(jax.ShapeDtypeStruct(shape, BF16 if shift else F32) for shift in range(count))


def per_device(
    hidden_in,
    resid_in,
    route_ids,
    route_weight,
    returns,
    run_moments,
    gate_w,
    up_w,
    down_w,
    value_w,
):
    groups = lax.axis_size("expert")
    side_y, side_x = lax.axis_size("y"), lax.axis_size("x")
    core = lax.axis_index("core")
    tok_rows, width = hidden_in.shape
    routes = route_ids.shape[1]
    cap = 3 * tok_rows * routes // (2 * groups)
    slot_total = groups * cap
    bins = value_w.shape[1]
    gate_w, up_w, down_w = gate_w[0], up_w[0], down_w[0]
    ff = gate_w.shape[1]
    own_rows = width // (side_y * side_x * 2)
    token_count = float(tok_rows * groups * side_y * side_x * 2)
    sds = jax.ShapeDtypeStruct
    anywhere = pl.BlockSpec(memory_space=pl.ANY)
    smem = pl.BlockSpec(memory_space=pltpu.SMEM)
    vmem = pl.BlockSpec(memory_space=pltpu.VMEM)

    coords = jnp.stack([lax.axis_index("x"), lax.axis_index("y")]).astype(jnp.int32)

    def core_half(array):
        blocks = array.reshape(side_y * side_x, 2, own_rows, array.shape[1])
        mine = pick(blocks, core, 1).reshape(width // 2, array.shape[1])
        other = pick(blocks, 1 - core, 1).reshape(width // 2, array.shape[1])
        return mine, other

    def exchange(blocks):
        return lax.all_to_all(blocks, "expert", 0, 0, tiled=True)

    def exchange_rows(rows):
        return exchange(rows.reshape(groups, cap, rows.shape[1])).reshape(rows.shape)

    outgoing, slots, placed_any = pl.pallas_call(
        lambda *refs: slots_kernel(groups, cap, *refs),
        out_shape=(
            sds((slot_total, width), BF16),
            sds((routes, tok_rows), jnp.int32),
            sds((slot_total, tok_rows), BF16),
        ),
        compiler_params=params(),
        cost_estimate=cost(2 * tok_rows * slot_total * width, 2 * width * (slot_total + tok_rows)),
        name="slots",
    )(route_ids.T, hidden_in)
    in_rows = exchange_rows(outgoing)

    with jax.named_scope("moments"):
        sums = jnp.stack([jnp.sum(returns), jnp.sum(returns * returns)])
        for axis_name in ("x", "y", "core"):
            sums = lax.psum(sums, axis_name)

    with jax.named_scope("weights_only"):
        mix = dot(down_w, value_w).astype(BF16)
        resid_logits = dot(resid_in, value_w)
        value_mine, _ = core_half(value_w)
        down_mine, _ = core_half(down_w.T)
        resid_mine, resid_other = core_half(resid_in.T)
        resid_peer = swap_cores(resid_other)

    steps = 1
    part = ff // steps
    act, one, two, route_logits = pl.pallas_call(
        lambda *refs: front_kernel(cap, *refs),
        grid=(steps,),
        in_specs=[
            whole((slot_total, width)),
            pl.BlockSpec((width, part), lambda j: (0, j)),
            pl.BlockSpec((width, part), lambda j: (0, j)),
            pl.BlockSpec((part, bins), lambda j: (j, 0)),
            smem,
        ]
        + [anywhere] * 4,
        out_specs=[
            pl.BlockSpec((slot_total, part), lambda j: (0, j)),
            pl.BlockSpec((slot_total, part), lambda j: (0, j)),
            pl.BlockSpec((slot_total, part), lambda j: (0, j)),
            whole((groups, cap + STAT_ROWS, bins)),
        ],
        out_shape=(
            sds((slot_total, ff), BF16),
            sds((slot_total, ff), BF16),
            sds((slot_total, ff), BF16),
            sds((groups, cap + STAT_ROWS, bins), BF16),
        ),
        scratch_shapes=[pltpu.VMEM((slot_total, bins), F32)],
        compiler_params=params(),
        cost_estimate=cost(4 * slot_total * width * ff, 4 * width * ff),
        name="front",
    )(in_rows, gate_w, up_w, mix, sums, value_mine, down_mine, resid_mine, resid_peer)
    back_logits = exchange(route_logits)
    with jax.named_scope("turned"):
        chips = side_y * side_x
        rows_mine, rows_other = pl.pallas_call(
            turn_kernel,
            grid=(4,),
            in_specs=[
                smem,
                pl.BlockSpec((slot_total, width // 4), lambda i: (0, i)),
                anywhere,
            ],
            out_specs=[pl.BlockSpec((chips // 4, own_rows, slot_total), lambda i: (i, 0, 0))] * 2,
            out_shape=(sds((chips, own_rows, slot_total), BF16),) * 2,
            compiler_params=params(),
            cost_estimate=cost(0, 4 * slot_total * width),
            name="turn",
        )(core.astype(jnp.int32)[None], in_rows, act)
        rows_mine = rows_mine.reshape(width // 2, slot_total)
        rows_peer = swap_cores(rows_other).reshape(width // 2, slot_total)
        act_peer, one_peer, two_peer = swap_cores(act), swap_cores(one), swap_cores(two)

    out_grad, logit_grad, grad_route = pl.pallas_call(
        lambda *refs: head_kernel(cap, token_count, *refs),
        in_specs=[smem]
        + [vmem] * 5
        + [anywhere] * 2
        + [smem],
        out_shape=(
            sds((slot_total, bins), BF16),
            sds((tok_rows, bins), BF16),
            sds((tok_rows, routes), F32),
        ),
        compiler_params=params(),
        cost_estimate=cost(8 * tok_rows * slot_total * bins, 4 * slot_total * bins),
        name="head",
    )(
        run_moments, back_logits, slots, route_weight, resid_logits, returns.reshape(tok_rows, 1),
        rows_mine, rows_other, coords,
    )
    row_grad = exchange_rows(out_grad)
    grad_peer = swap_cores(logit_grad)

    row_grad_peer = swap_cores(row_grad)

    strip = min(1024, width)
    input_grad, pair = pl.pallas_call(
        back_kernel,
        grid=(width // strip,),
        in_specs=[
            whole((slot_total, bins)),
            whole((ff, bins)),
            whole((slot_total, ff)),
            whole((slot_total, ff)),
            pl.BlockSpec((strip, ff), lambda i: (i, 0)),
            pl.BlockSpec((strip, ff), lambda i: (i, 0)),
        ]
        + [anywhere] * 5,
        out_specs=[
            pl.BlockSpec((slot_total, strip), lambda i: (0, i)),
            whole((slot_total, 2 * ff)),
        ],
        out_shape=(
            sds((slot_total, width), BF16),
            sds((slot_total, 2 * ff), BF16),
        ),
        compiler_params=params(),
        cost_estimate=cost(4 * slot_total * width * ff, 4 * width * ff),
        name="back",
    )(
        row_grad, mix, one, two, gate_w, up_w, rows_peer, grad_peer, act_peer, one_peer, two_peer
    )
    back_grad = exchange_rows(input_grad)

    half = width // 2
    cut = ff // 6
    first_columns, second_columns = ff + cut + bins, 2 * ff - cut
    first_block, second_block = (side_y, own_rows, first_columns), (side_x, own_rows, second_columns)

    def parts(kernel, shifts, blocked, shared, outs, name):
        def shift_of(step):
            return shifts[0] if len(shifts) == 1 else shifts[0] + step * (shifts[1] - shifts[0])

        def tall(depth):
            return pl.BlockSpec(
                (side_y, 1, own_rows, depth),
                lambda step, at: (0, lax.rem(at[0] + shift_of(step), side_x), 0, 0),
            )

        def wide(depth):
            return pl.BlockSpec(
                (1, side_x, own_rows, depth),
                lambda step, at: (lax.rem(at[1] + shift_of(step), side_y), 0, 0, 0),
            )

        makes = {"x": tall, "y": wide}
        return pl.pallas_call(
            kernel,
            grid_spec=pltpu.PrefetchScalarGridSpec(
                num_scalar_prefetch=1,
                grid=(len(shifts),),
                in_specs=[makes[along](rows.shape[1]) for along, rows in blocked]
                + [whole(item.shape) if spec is None else spec for spec, item in shared],
                out_specs=[whole(out.shape) for out in outs],
            ),
            out_shape=outs,
            compiler_params=params(),
            cost_estimate=cost(len(shifts) * half * slot_total * ff, len(shifts) * 3 * MIB),
            name=name,
        )(
            coords,
            *[rows.reshape(side_y, side_x, own_rows, rows.shape[1]) for _, rows in blocked],
            *[item for _, item in shared],
        )

    def step_on(array, axis_name, shift):
        size = lax.axis_size(axis_name)
        return lax.ppermute(array, axis_name, [(k, (k + shift) % size) for k in range(size)])

    x_rows = [
        ("x", r) for r in (rows_mine, rows_peer, resid_mine, resid_peer, down_mine, value_mine)
    ]
    y_rows = [("y", r) for r in (rows_mine, rows_peer, value_mine)]
    first_out, second_out = sds(first_block, BF16), sds(second_block, BF16)
    first_far, second_far, pair_peer, inner = parts(
        far_kernel,
        (2,),
        x_rows + y_rows,
        [
            (None, item)
            for item in (
                pair, logit_grad, grad_peer, row_grad, row_grad_peer, mix, one_peer, two_peer,
                act, act_peer,
            )
        ],
        [first_out, second_out, sds(pair.shape, BF16), sds((ff, bins), BF16)],
        "far",
    )
    gate_spec = pl.BlockSpec((slot_total, ff), lambda *_: (0, 0))
    up_spec = pl.BlockSpec((slot_total, ff), lambda *_: (0, 1))

    firsts = [step_on(first_far, "x", 2)]
    seconds = [step_on(second_far, "y", 2)]
    first_up, first_down = parts(
        lambda *refs: x_kernel(2, *refs),
        (1, 3),
        x_rows,
        [
            (gate_spec, pair), (gate_spec, pair_peer), (None, inner), (None, logit_grad),
            (None, grad_peer),
        ],
        [first_out] * 2,
        "x_near",
    )
    firsts += [step_on(first_up, "x", 1), step_on(first_down, "x", 3)]
    second_up, second_down = parts(
        lambda *refs: y_kernel(2, *refs),
        (1, 3),
        y_rows,
        [
            (up_spec, pair), (up_spec, pair_peer), (None, inner), (anywhere, first_up),
        ],
        [second_out] * 2,
        "y_near",
    )
    first_own, second_own = parts(
        own_kernel,
        (0,),
        x_rows + y_rows,
        [
            (None, pair), (None, pair_peer), (None, inner), (None, logit_grad), (None, grad_peer),
            (anywhere, second_up), (anywhere, seconds[0]), (anywhere, firsts[0]),
        ],
        [first_out, second_out],
        "own",
    )
    seconds += [step_on(second_up, "y", 1), step_on(second_down, "y", 3)]

    head, *firsts = pl.pallas_call(
        first_kernel,
        in_specs=[smem] + [vmem] * 4,
        out_shape=(sds((side_y, own_rows, bins), F32),)
        + per_shift(side_y, (own_rows, first_columns - bins)),
        compiler_params=params(),
        cost_estimate=cost(0, 12 * side_y * own_rows * ff),
        name="first",
    )(coords, first_own, *firsts)
    first_came = send(firsts, "y")
    seconds = pl.pallas_call(
        second_kernel,
        in_specs=[smem] + [vmem] * 4,
        out_shape=per_shift(side_x, (own_rows, second_columns)),
        compiler_params=params(),
        cost_estimate=cost(0, 24 * side_y * own_rows * ff),
        name="second",
    )(coords, second_own, *seconds)
    second_came = send(seconds, "x")
    with jax.named_scope("hidden"):
        grad_hidden = dot(placed_any, back_grad, 0, 0).astype(BF16)
    head = pl.pallas_call(
        pass_kernel,
        in_specs=[anywhere] * 2,
        out_specs=anywhere,
        out_shape=sds(head.shape, F32),
        input_output_aliases={0: 0},
        compiler_params=params(),
        cost_estimate=cost(0, 8 * side_y * own_rows * bins),
        name="pass",
    )(head, back_grad)
    shares = head.reshape(side_y * groups, own_rows // groups, bins)
    shares = lax.all_to_all(shares, ("y", "expert"), 0, 0, tiled=True)
    grad_gate, grad_up, grad_down, grad_value = pl.pallas_call(
        lambda *refs: last_kernel(side_x, side_y, *refs),
        out_shape=(
            sds((own_rows, ff), F32),
            sds((own_rows, ff), F32),
            sds((own_rows, ff), F32),
            sds(shares.shape[1:], F32),
        ),
        compiler_params=params(),
        cost_estimate=cost(0, 24 * own_rows * ff),
        name="last",
    )(shares, firsts[0], *first_came, seconds[0], *second_came)
    return (grad_hidden, grad_route, grad_gate[None], grad_up[None], grad_down.T[None], grad_value)


def solution(mesh):
    pair = 2
    plane = mesh.shape["dp"] // pair
    side = math.isqrt(plane)
    grid = Mesh(mesh.devices.reshape(plane // side, side, pair, mesh.shape["expert"]), ALL)
    rows = P(ALL, None)
    dp = ("y", "x", "core")
    in_specs = (
        rows,
        rows,
        rows,
        rows,
        P(ALL),
        P(),
        P("expert", None, None),
        P("expert", None, None),
        P("expert", None, None),
        P(),
    )
    out_specs = (
        rows,
        rows,
        P("expert", dp, None),
        P("expert", dp, None),
        P("expert", None, dp),
        rows,
    )
    return jax.shard_map(
        per_device, mesh=grid, in_specs=in_specs, out_specs=out_specs, check_vma=False
    )
```
